32 devices in a mesh: dp: 8 (over z, x), tensor: 4 (over y, core).
Axes of the slice: x: 2, y: 2, z: 4, core: 2. Of those that a mesh axis runs over, the one named last changes fastest.
Arguments:
- series: bfloat16 [32, 864, 96], P('dp', 'tensor'), may hold values from -6 to 6
- embed_weight: bfloat16 [96, 512], replicated, may hold values from -0.625 to 0.625
- embed_bias: float32 [512], replicated, may hold values from -3 to 3
- query_weight: bfloat16 [512, 512], replicated, may hold values from -0.25 to 0.25
- query_bias: float32 [512], replicated, may hold values from -1.75 to 1.75
- key_weight: bfloat16 [512, 512], replicated, may hold values from -0.25 to 0.25
- value_weight: bfloat16 [512, 512], replicated, may hold values from -0.25 to 0.25
- value_bias: float32 [512], replicated, may hold values from -0.1875 to 0.1875
- out_weight: bfloat16 [512, 512], replicated, may hold values from -3 to 3
- out_bias: float32 [512], replicated, may hold values from -1.75 to 1.75
- first_gain: float32 [512], replicated, may hold values from 0.25 to 1.75
- first_shift: float32 [512], replicated, may hold values from -1.75 to 1.75
- up_weight: bfloat16 [2048, 512], P('tensor'), may hold values from -0.25 to 0.25
- up_bias: bfloat16 [2048], P('tensor'), may hold values from -1.75 to 1.75
- down_weight: bfloat16 [2048, 512], P('tensor'), may hold values from -0.125 to 0.125
- down_bias: float32 [512], replicated, may hold values from -1.75 to 1.75
- second_gain: float32 [512], replicated, may hold values from 0.25 to 1.75
- second_shift: float32 [512], replicated, may hold values from -1.75 to 1.75
- cotangent: bfloat16 [32, 864, 512], P('dp', 'tensor'), may hold values from -8 to 8
Outputs:
- mixed_out: bfloat16 [32, 864, 512], P('dp', 'tensor')
- series_grad: bfloat16 [32, 864, 96], P('dp', 'tensor')
- embed_weight_grad: float32 [96, 512], replicated
- embed_bias_grad: float32 [512], replicated
- query_weight_grad: float32 [512, 512], replicated
- query_bias_grad: float32 [512], replicated
- key_weight_grad: float32 [512, 512], replicated
- value_weight_grad: float32 [512, 512], replicated
- value_bias_grad: float32 [512], replicated
- out_weight_grad: float32 [512, 512], replicated
- out_bias_grad: float32 [512], replicated
- first_gain_grad: float32 [512], replicated
- first_shift_grad: float32 [512], replicated
- up_weight_grad: float32 [2048, 512], P('tensor', 'dp')
- up_bias_grad: float32 [2048], replicated
- down_weight_grad: float32 [2048, 512], P('tensor', 'dp')
- down_bias_grad: float32 [512], replicated
- second_gain_grad: float32 [512], replicated
- second_shift_grad: float32 [512], replicated
The draws below stay inside these ranges and needn't reach their ends.
All inputs are finite; a program needn't handle non-finite values.
Results may differ from the reference program's by a relative error of at most 0.02.
Values may be sent and summed in bfloat16 or wider, within the bound.
A program may use at most 128 MiB of HBM per device.

```python
import math
import jax
import jax.numpy as jnp
from jax import lax

D = 512
HEADS = 8
FF = 2048
LOOKBACK = 96
VARIATES = 864
WINDOWS = 32


def raised(array, own_key, source, target, blocks, factor):
    owner, partner = [(jnp.arange(array.shape[dim]) // (array.shape[dim] // blocks)).reshape([-1 if axis == dim else 1 for axis in range(array.ndim)]) for dim in (source, target)]
    chosen = jax.random.permutation(own_key, blocks)[partner]
    strong = (owner == chosen) | (owner == (partner + blocks // 2) % blocks)
    return jnp.where(strong, factor * array, array)


def block_scale(rng, extent, split, low, top_value):
    def one(position, blocks):
        draws = jax.random.uniform(jax.random.fold_in(jax.random.fold_in(rng, 6), position), (blocks,), jnp.float32, low / len(split), top_value / len(split))
        return jnp.repeat(jnp.exp(draws), extent[position] // blocks).reshape((-1,) + (1,) * (len(extent) - position - 1))

    factor_of = one(*split[0])
    for cut in split[1:]:
        factor_of = factor_of * one(*cut)
    return factor_of


def bell_draw(rng, extent, scale, limit, split=(), dtype=jnp.bfloat16):
    factor_of = block_scale(rng, extent, split, -0.22, 0.18) if split else 1.0
    entries = jax.random.normal(rng, extent, jnp.float32) * scale * factor_of
    return jnp.minimum(jnp.maximum(entries, -limit), limit).astype(dtype)


def gaussian_with(key, dims, scale, reach, cuts, heavy, held_as=jnp.bfloat16):
    values = scale * jax.random.normal(key, dims, jnp.float32)
    if cuts:
        values = values * block_scale(key, dims, cuts, -0.22, 0.18)
    return jnp.clip(raised(values, jax.random.fold_in(key, 3), *heavy), -reach, reach).astype(held_as)


def setup_inputs(seed: int = 0) -> dict:
    key_of = jax.random.split(jax.random.key(seed), 20)
    series = bell_draw(key_of[0], (WINDOWS, VARIATES, LOOKBACK), 1.0, 6.0, ((0, 8), (1, 4)))
    embed_weight = bell_draw(key_of[1], (LOOKBACK, D), LOOKBACK ** -0.5, 0.625)
    embed_bias = bell_draw(key_of[2], (D,), 0.5, 3.0, (), jnp.float32)
    query_weight = bell_draw(key_of[3], (D, D), D ** -0.5, 0.25)
    query_bias = bell_draw(key_of[4], (D,), 0.3, 1.75, (), jnp.float32)
    key_weight = bell_draw(key_of[5], (D, D), D ** -0.5, 0.25)
    value_weight = bell_draw(key_of[6], (D, D), D ** -0.5, 0.25)
    value_bias = bell_draw(key_of[7], (D,), 0.03, 0.1875, (), jnp.float32)
    out_weight = bell_draw(key_of[8], (D, D), 4 ** -0.5, 3.0)
    out_bias = bell_draw(key_of[9], (D,), 0.3, 1.75, (), jnp.float32)
    first_gain = jnp.clip(1.0 + 0.15 * jax.random.normal(key_of[10], (D,), jnp.float32), 0.25, 1.75)
    first_shift = bell_draw(key_of[11], (D,), 0.3, 1.75, (), jnp.float32)
    up_weight = bell_draw(key_of[12], (FF, D), D ** -0.5, 0.25, ((0, 4),))
    up_bias = bell_draw(key_of[13], (FF,), 0.3, 1.75, ((0, 4),))
    down_weight = bell_draw(key_of[14], (FF, D), FF ** -0.5, 0.125, ((0, 4),))
    down_bias = bell_draw(key_of[15], (D,), 0.3, 1.75, (), jnp.float32)
    second_gain = jnp.clip(1.0 + 0.15 * jax.random.normal(key_of[16], (D,), jnp.float32), 0.25, 1.75)
    second_shift = bell_draw(key_of[17], (D,), 0.3, 1.75, (), jnp.float32)
    cotangent = gaussian_with(key_of[18], (WINDOWS, VARIATES, D), 1.0, 8.0, ((0, 8), (1, 4)), (0, 2, 8, 2.0))
    return {"series": series, "embed_weight": embed_weight, "embed_bias": embed_bias, "query_weight": query_weight, "query_bias": query_bias, "key_weight": key_weight, "value_weight": value_weight, "value_bias": value_bias, "out_weight": out_weight, "out_bias": out_bias, "first_gain": first_gain, "first_shift": first_shift, "up_weight": up_weight, "up_bias": up_bias, "down_weight": down_weight, "down_bias": down_bias, "second_gain": second_gain, "second_shift": second_shift, "cotangent": cotangent}


EPSILON = 1e-05
HIGHEST_PRECISION = lax.Precision.HIGHEST

@jax.custom_vjp
def low(v):
    return lax.optimization_barrier(v.astype(jnp.bfloat16)).astype(jnp.float32)

@jax.custom_vjp
def low_back(v):
    return v

def low_keep(v):
    return (low(v), None)

def low_pass(kept, grad):
    return (grad,)

def back_keep(v):
    return (v, None)

def back_low(kept, grad):
    return (low(grad),)
low.defvjp(low_keep, low_pass)
low_back.defvjp(back_keep, back_low)

def rounded(value):
    return low(low_back(value))

def norm_rows(row_values, norm_gain, norm_shift):
    average = lax.optimization_barrier(jnp.mean(row_values, axis=-1, keepdims=True))
    centred = row_values - average
    variance = lax.optimization_barrier(jnp.mean(centred * centred, axis=-1, keepdims=True))
    return centred * lax.rsqrt(variance + EPSILON) * norm_gain + norm_shift

def window_layer(weights, block_series):
    embed_weight, embed_bias, query_weight, query_bias, key_weight, value_weight, value_bias, out_weight, out_bias, first_gain, first_shift, up_weight, up_bias, down_weight, down_bias, second_gain, second_shift = weights
    group_size, variates, _ = block_series.shape
    model_width = embed_weight.shape[1]
    head_size = model_width // HEADS
    factor = head_size ** (-0.5)
    embedded = low_back(jnp.einsum('gvp,pd->gvd', block_series, embed_weight, precision=HIGHEST_PRECISION) + embed_bias)
    embedded_low = low(embedded)
    queries = rounded(jnp.einsum('gvd,de->gve', embedded_low, query_weight, precision=HIGHEST_PRECISION) + query_bias)
    keys_raw = rounded(jnp.einsum('gvd,de->gve', embedded_low, key_weight, precision=HIGHEST_PRECISION))
    values_raw = rounded(jnp.einsum('gvd,de->gve', embedded_low, value_weight, precision=HIGHEST_PRECISION) + value_bias)
    queries = queries.reshape(group_size, variates, HEADS, head_size)
    keys_raw = keys_raw.reshape(group_size, variates, HEADS, head_size)
    values_raw = values_raw.reshape(group_size, variates, HEADS, head_size)
    scores = low_back(jnp.einsum('gqhe,gkhe->ghqk', queries, keys_raw, precision=HIGHEST_PRECISION) * factor)
    probability = jax.nn.softmax(scores, axis=-1)
    mixed = rounded(jnp.einsum('ghqk,gkhe->gqhe', low(probability), values_raw, precision=HIGHEST_PRECISION))
    mixed = mixed.reshape(group_size, variates, model_width)
    attended = low_back(jnp.einsum('gvd,de->gve', mixed, out_weight, precision=HIGHEST_PRECISION) + out_bias)
    first_out = norm_rows(embedded + attended, first_gain, first_shift)
    pre_hidden = low_back(jnp.einsum('gvd,fd->gvf', low(first_out), up_weight, precision=HIGHEST_PRECISION) + up_bias)
    hidden = low(jax.nn.gelu(pre_hidden))
    branch = low_back(jnp.einsum('gvf,fd->gvd', hidden, down_weight, precision=HIGHEST_PRECISION) + down_bias)
    return norm_rows(first_out + branch, second_gain, second_shift)

def reference(series, embed_weight, embed_bias, query_weight, query_bias, key_weight, value_weight, value_bias, out_weight, out_bias, first_gain, first_shift, up_weight, up_bias, down_weight, down_bias, second_gain, second_shift, cotangent):
    params = tuple((argument.astype(jnp.float32) for argument in (embed_weight, embed_bias, query_weight, query_bias, key_weight, value_weight, value_bias, out_weight, out_bias, first_gain, first_shift, up_weight, up_bias, down_weight, down_bias, second_gain, second_shift)))
    grouping = math.gcd(WINDOWS, 4)

    def whole_layer(weights, inputs):
        blocks = inputs.reshape(WINDOWS // grouping, grouping, VARIATES, LOOKBACK)

        def one_block(block_series):
            return jax.checkpoint(window_layer)(weights, block_series)
        outputs = lax.map(one_block, blocks)
        return outputs.reshape(WINDOWS, VARIATES, outputs.shape[-1])
    mixed_out, pullback = jax.vjp(whole_layer, params, series.astype(jnp.float32))
    gradients, series_grad = pullback(cotangent.astype(jnp.float32))
    return (mixed_out.astype(jnp.bfloat16), series_grad.astype(jnp.bfloat16), gradients[0], gradients[1], gradients[2], gradients[3], gradients[4], gradients[5], gradients[6], gradients[7], gradients[8], gradients[9], gradients[10], gradients[11], gradients[12], gradients[13], gradients[14], gradients[15], gradients[16])
```

```python
import functools
import jax
import jax.numpy as jnp
from jax import lax
from jax.experimental import pallas as pl
from jax.experimental.pallas import tpu as pltpu
from jax.sharding import PartitionSpec as P

HEADS = 8
EPSILON = 1e-05
F32 = jnp.float32
BF16 = jnp.bfloat16
MESH = pl.DeviceIdType.MESH
GELU_A = 0.7978845608028654
GELU_B = GELU_A * 0.044715
MASKED = -1e30

EMBED, QUERY, VALUE, OUT, GAIN1, SHIFT1, DOWN, GAIN2, SHIFT2, UP = range(10)


def mm(left, right, cl=1, cr=0):
    return lax.dot_general(
        left, right, (((cl,), (cr,)), ((), ())), preferred_element_type=F32
    )


def row_mean(x):
    return jnp.mean(x, axis=1, keepdims=True)


def col_sum(x):
    return jnp.sum(x, axis=0, keepdims=True)


def pad_rows(x, rows):
    if x.shape[0] == rows:
        return x
    return jnp.concatenate([x, jnp.zeros((rows - x.shape[0], x.shape[1]), x.dtype)], axis=0)


class Sems:
    def __init__(self, send, recv):
        self.send, self.recv, self.used = send, recv, 0

    def copy(self, src, dst, device):
        i = self.used
        self.used += 1
        return pltpu.make_async_remote_copy(
            src_ref=src,
            dst_ref=dst,
            send_sem=self.send.at[i],
            recv_sem=self.recv.at[i],
            device_id=device,
            device_id_type=MESH,
        )

    def local(self, src, dst):
        i = self.used
        self.used += 1
        return pltpu.make_async_copy(src, dst, self.send.at[i])

    def slot(self):
        i = self.used
        self.used += 1
        return self.send.at[i], self.recv.at[i]


N_SEMS = 160
DIRECT = 4


def doublings(nz):
    assert nz & (nz - 1) == 0
    return nz.bit_length() - 1


def kernel(
    cfg,
    series, cot_in, w_embed, w_q, w_k, w_v, w_o, w_up, w_down, vec, ub_in,
    o_mixed, o_series, o_qkv, o_out, o_up, o_down, o_tail,
    xs, xp, en, elow, qkv, prob, ds, mxf, mx, rinv, inv1, flow, hid, slope, cot, g2, gb,
    qt, dt, wb, wqkv, wo, we, ubb,
    g, rc, r1, r2, rz,
    gq, rcq, r1q, r2q, rzq,
    go, rco, r1o, r2o, rzo,
    tb, rt, rtz,
    bv, send, recv,
):
    blocks, rows, padded, nz, fr = cfg
    n = blocks * padded
    width = wo.shape[0]
    pairs = qkv.shape[0]
    dp, t = lax.axis_index("dp"), lax.axis_index("tensor")
    c, y = t % 2, t // 2
    b, z = dp % 2, dp // 2
    co, yo, bo = 1 - c, 1 - y, 1 - b
    sems = Sems(send, recv)

    def dev(cc, yy, bb, zz=None):
        return ((z if zz is None else zz) * 2 + bb, yy * 2 + cc)

    core_dev, y_dev, x_dev = dev(co, y, b), dev(c, yo, b), dev(c, y, bo)
    peers = []
    for k in range(1, 8):
        peers.append((
            co if k & 4 else c,
            yo if k & 2 else y,
            bo if k & 1 else b,
        ))

    barrier = pltpu.get_barrier_semaphore()
    for pc, py, pb in peers:
        pl.semaphore_signal(barrier, inc=1, device_id=dev(pc, py, pb), device_id_type=MESH)
    for k in range(1, nz):
        pl.semaphore_signal(
            barrier, inc=1, device_id=dev(c, y, b, (z + k) % nz), device_id_type=MESH
        )

    load_we = sems.local(w_embed, we)
    load_we.start()
    own_x = sems.local(series.at[t], xs.at[t])
    own_x.start()
    load_qkv = []
    for p in range(pairs):
        for j, w in enumerate((w_q, w_k, w_v)):
            cp = sems.local(
                w.at[:, 128 * p:128 * p + 128], wqkv.at[p, :, 128 * j:128 * j + 128]
            )
            cp.start()
            load_qkv.append(cp)
    load_wo = sems.local(w_o, wo)
    load_wo.start()
    own_w = [sems.local(w, wb.at[m, t]) for m, w in enumerate((w_up, w_down))]
    for cp in own_w:
        cp.start()
    own_cot = sems.local(cot_in.at[t], cot.at[t])
    own_cot.start()
    ubb[t] = ub_in[...]
    bv[...] = jnp.zeros_like(bv)

    pl.semaphore_wait(barrier, 7 + nz - 1)

    def exchange(src, dst):
        out = []
        for k in range(1, blocks):
            other = (t + k) % blocks
            out.append(sems.copy(src.at[other], dst.at[t], (dp, other)))
        return out

    send_x = exchange(series, xs)
    for cp in send_x:
        cp.start()

    hidden = w_up.shape[0]
    part = hidden // 4
    t_y = yo * 2 + c
    stage_y = []
    for m, w in enumerate((w_up, w_down)):
        for s in range(2):
            at = pl.ds(pl.multiple_of(b * 2 * part + s * part, part), part)
            stage_y.append((m, at, sems.copy(w.at[at], wb.at[m, t, at], y_dev)))
    for _, _, cp in stage_y:
        cp.start()
    stage_core = [
        sems.copy(w, wb.at[m, t], core_dev) for m, w in enumerate((w_up, w_down))
    ]
    for cp in stage_core:
        cp.start()
    stage_ub = []
    for k in range(1, blocks):
        other = (t + k) % blocks
        stage_ub.append(sems.copy(ub_in, ubb.at[t], (dp, other)))
    for cp in stage_ub:
        cp.start()

    stage_x, stage_d, stage_e = [], [], []

    def weights_forward_y():
        for m, at, cp in stage_y:
            cp.wait_recv()
            nxt = sems.copy(wb.at[m, t_y, at], wb.at[m, t_y, at], x_dev)
            nxt.start()
            stage_x.append((m, nxt))
            fwd = sems.copy(wb.at[m, t_y, at], wb.at[m, t_y, at], core_dev)
            fwd.start()
            stage_d.append(fwd)

    def weights_forward_x():
        for i, (m, cp) in enumerate(stage_x):
            cp.wait_recv()
            s = i % 2
            at = pl.ds(pl.multiple_of(bo * 2 * part + s * part, part), part)
            fwd = sems.copy(wb.at[m, t_y, at], wb.at[m, t_y, at], core_dev)
            fwd.start()
            stage_e.append(fwd)

    def weights_ready():
        for cp in own_w:
            cp.wait()
        for cp in stage_core + stage_ub + stage_d + stage_e:
            cp.wait_recv()
        for cp in stage_core + stage_ub + stage_d + stage_e:
            cp.wait_send()
        for _, _, cp in stage_y:
            cp.wait_send()
        for _, cp in stage_x:
            cp.wait_send()

    load_we.wait()
    own_x.wait()
    for cp in send_x:
        cp.wait()
    for i in range(blocks):
        x = xs[i]
        e = mm(x, we[...]) + vec[EMBED:EMBED + 1, :]
        at = pl.ds(i * padded, padded)
        e = pad_rows(e, padded)
        en[at, :] = e
        elow[at, :] = e.astype(BF16)
        xp[at, :] = pad_rows(x.astype(F32), padded).astype(BF16)
    for cp in load_qkv:
        cp.wait()

    def project(p, carry):
        lanes = pl.ds(pl.multiple_of(p * 128, 128), 128)
        out = mm(elow[...], wqkv[p])
        q = (out[:, :128] + vec[QUERY:QUERY + 1, lanes]).astype(BF16)
        qkv[p, :, 0:128] = q * jnp.asarray(0.125, BF16)
        qkv[p, :, 128:256] = out[:, 128:256].astype(BF16)
        qkv[p, :, 256:384] = (out[:, 256:384] + vec[VALUE:VALUE + 1, lanes]).astype(BF16)
        qkv[p, :, 384:512] = jnp.ones((n, 128), BF16)
        return carry

    lax.fori_loop(0, pairs, project, 0)

    weights_forward_y()
    send_cot = exchange(cot_in, cot)
    for cp in send_cot:
        cp.start()

    lane = lax.broadcasted_iota(jnp.int32, (1, 128), 1)
    key_at = lax.broadcasted_iota(jnp.int32, (1, n), 1)
    mask = jnp.where(key_at % padded >= rows, MASKED, 0.0).astype(F32)

    tile_f = 128

    def attend_pair(p):
        def attend_tile(i, carry):
            at = pl.ds(pl.multiple_of(i * tile_f, tile_f), tile_f)
            q = qkv[p, at, 0:128]
            outs, inverses = [], []
            for h in range(2):
                qm = jnp.where((lane // 64) == h, q, jnp.zeros_like(q))
                s = mm(qm, qkv[p, :, 128:256], 1, 1) + mask
                e = jnp.exp(s - jnp.max(s, axis=1, keepdims=True)).astype(BF16)
                prob[2 * p + h, at, :] = e
                o = mm(e, qkv[p, :, 256:512])
                outs.append(o[:, :128])
                inverses.append(1.0 / o[:, 128:])
            inverse = jnp.where(lane < 64, inverses[0], inverses[1])
            o = jnp.where(lane < 64, outs[0], outs[1]) * inverse
            lanes = pl.ds(pl.multiple_of(p * 128, 128), 128)
            mxf[at, lanes] = o
            mx[at, lanes] = o.astype(BF16)
            rinv[at, lanes] = inverse.astype(BF16)
            return carry

        lax.fori_loop(0, n // tile_f, attend_tile, 0, unroll=True)

    def attend_some(p, carry):
        attend_pair(p)
        return carry

    lax.fori_loop(0, pairs - 1, attend_some, 0)
    weights_forward_x()
    lax.fori_loop(pairs - 1, pairs, attend_some, 0)

    load_wo.wait()

    def first_norm(i, carry):
        at = pl.ds(pl.multiple_of(i * padded, padded), padded)
        zz = en[at, :] + (mm(mx[at, :], wo[...]) + vec[OUT:OUT + 1, :])
        centred = zz - row_mean(zz)
        inv = lax.rsqrt(row_mean(centred * centred) + EPSILON)
        nn = centred * inv
        en[at, :] = nn
        inv1[at, :] = jnp.broadcast_to(inv, (padded, 128))
        flow[at, :] = (nn * vec[GAIN1:GAIN1 + 1, :] + vec[SHIFT1:SHIFT1 + 1, :]).astype(BF16)
        return carry

    lax.fori_loop(0, blocks, first_norm, 0)
    weights_ready()
    own_cot.wait()
    for cp in send_cot:
        cp.wait()

    def feed_forward(i, carry):
        at = pl.ds(pl.multiple_of(i * padded, padded), padded)
        fl = flow[at, :]
        acc = en[at, :] * vec[GAIN1:GAIN1 + 1, :] + vec[SHIFT1:SHIFT1 + 1, :]
        acc = acc + vec[DOWN:DOWN + 1, :]
        for j in range(blocks):
            v = mm(fl, wb[0, j], 1, 1) + ubb[j, 0:1, :]
            v2 = v * v
            half = 0.5 * jnp.tanh(v * (GELU_A + GELU_B * v2)) + 0.5
            h = v * half
            slope[j, at, :] = (
                half + h * (1.0 - half) * (2 * GELU_A + (6 * GELU_B) * v2)
            ).astype(BF16)
            h = h.astype(BF16)
            hid[j, at, :] = h
            acc = acc + mm(h, wb[1, j])
        centred = acc - row_mean(acc)
        inv = lax.rsqrt(row_mean(centred * centred) + EPSILON)
        nn = centred * inv
        up = pad_rows(cot[i].astype(F32), padded)
        result = nn * vec[GAIN2:GAIN2 + 1, :] + vec[SHIFT2:SHIFT2 + 1, :]
        cot[i] = result[:rows].astype(BF16)
        gg = up * vec[GAIN2:GAIN2 + 1, :]
        back = inv * (gg - row_mean(gg) - nn * row_mean(gg * nn))
        g2[at, :] = back
        low = back.astype(BF16)
        gb[at, :] = low
        bv[GAIN2:GAIN2 + 1, :] += col_sum(up * nn)
        bv[SHIFT2:SHIFT2 + 1, :] += col_sum(up)
        bv[DOWN:DOWN + 1, :] += col_sum(low.astype(F32))
        return carry

    lax.fori_loop(0, blocks, feed_forward, 0)

    own_mixed = sems.local(cot.at[t], o_mixed.at[t])
    own_mixed.start()
    send_mixed = exchange(cot, o_mixed)
    for cp in send_mixed:
        cp.start()

    def add_into(dst, src, index):
        dst[index] = (dst[index].astype(F32) + src[...].astype(F32)).astype(BF16)

    class FeedSum:
        def __init__(self, m, out):
            self.m, self.out = m, out

        def core(self):
            m = self.m
            self.cps = []
            for yy in range(2):
                cp = sems.copy(g.at[m, yy * 2 + co], rc.at[m, yy], core_dev)
                cp.start()
                self.cps.append(cp)

        def first(self):
            m = self.m
            for yy, cp in enumerate(self.cps):
                cp.wait()
                for bb in range(2):
                    for zz in range(nz):
                        add_into(g, rc.at[m, yy, bb, zz], (m, yy * 2 + c, bb, zz))
            self.cps = []
            if m == 1:
                cp = sems.copy(g.at[m, yo * 2 + c], r1.at[m], y_dev)
                cp.start()
                self.cps.append(cp)
            else:
                for yy in range(2):
                    cp = sems.copy(g.at[m, yy * 2 + c, bo], r1.at[m, yy], x_dev)
                    cp.start()
                    self.cps.append(cp)

        def second(self):
            m = self.m
            for cp in self.cps:
                cp.wait()
            if m == 1:
                for bb in range(2):
                    for zz in range(nz):
                        add_into(g, r1.at[m, bb, zz], (m, t, bb, zz))
                cp = sems.copy(g.at[m, t, bo], r2.at[m], x_dev)
            else:
                for yy in range(2):
                    for zz in range(nz):
                        add_into(g, r1.at[m, yy, zz], (m, yy * 2 + c, b, zz))
                cp = sems.copy(g.at[m, yo * 2 + c, b], r2.at[m], y_dev)
            cp.start()
            self.cps = [cp]

        def third(self):
            m = self.m
            for cp in self.cps:
                cp.wait()
            for zz in range(nz):
                add_into(g, r2.at[m, zz], (m, t, b, zz))
            self.cps = []
            for k in range(1, nz):
                zz = (z + k) % nz
                cp = sems.copy(g.at[m, t, b, zz], rz.at[m, k - 1], dev(c, y, b, zz))
                cp.start()
                self.cps.append(cp)

        def last(self):
            m = self.m
            for cp in self.cps:
                cp.wait()
            total = g[m, t, b, z].astype(F32)
            for k in range(nz - 1):
                total = total + rz[m, k].astype(F32)
            self.out[...] = total

    class MatrixSum:
        def __init__(self, grad, rcv, rcv1, rcv2, rcvz, out, y_first):
            self.refs = (grad, rcv, rcv1, rcv2, rcvz, out)
            self.y_first = y_first

        def start(self, src, dst, device):
            cp = sems.copy(src, dst, device)
            cp.start()
            self.cps.append(cp)

        def wait(self):
            for cp in self.cps:
                cp.wait()
            self.cps = []

        def steps(self):
            grad, rcv, rcv1, rcv2, rcvz, out = self.refs
            self.cps = []
            self.start(grad.at[co], rcv, core_dev)
            yield
            self.wait()
            for yy in range(2):
                for bb in range(2):
                    add_into(grad, rcv.at[yy, bb], (c, yy, bb))
            if self.y_first:
                self.start(grad.at[c, yo], rcv1, y_dev)
            else:
                for yy in range(2):
                    self.start(grad.at[c, yy, bo], rcv1.at[yy], x_dev)
            yield
            self.wait()
            for i in range(2):
                add_into(grad, rcv1.at[i], (c, y, i) if self.y_first else (c, i, b))
            if self.y_first:
                self.start(grad.at[c, y, bo], rcv2, x_dev)
            else:
                self.start(grad.at[c, yo, b], rcv2, y_dev)
            yield
            self.wait()
            add_into(grad, rcv2, (c, y, b))
            if nz <= DIRECT:
                rcvz[z] = grad[c, y, b]
                for k in range(1, nz):
                    self.start(grad.at[c, y, b], rcvz.at[z], dev(c, y, b, (z + k) % nz))
                yield
                self.wait()
                total = rcvz[0].astype(F32)
                for k in range(1, nz):
                    total = total + rcvz[k].astype(F32)
                out[c, y, b] = total.astype(BF16)
            else:
                for s in range(doublings(nz)):
                    far = z + 2**s * (1 - 2 * ((z // 2**s) % 2))
                    self.start(grad.at[c, y, b], rcvz.at[s], dev(c, y, b, far))
                    yield
                    self.wait()
                    add_into(grad, rcvz.at[s], (c, y, b))
                out[c, y, b] = grad[c, y, b]
            if self.y_first:
                self.start(out.at[c, y, b], out.at[c, y, b], x_dev)
            else:
                self.start(out.at[c, y, b], out.at[c, y, b], y_dev)
            yield
            self.wait()
            if self.y_first:
                self.start(out.at[c, y], out.at[c, y], y_dev)
            else:
                for yy in range(2):
                    self.start(out.at[c, yy, b], out.at[c, yy, b], x_dev)
            yield
            self.wait()
            self.start(out.at[c], out.at[c], core_dev)
            yield
            self.wait()

    down_sum, up_sum = FeedSum(0, o_down), FeedSum(1, o_up)

    def feed_grad(m, left, right):
        def one(j, carry):
            out = mm(left, right[j], 0, 0).astype(BF16)
            for zz in range(nz):
                for bb in range(2):
                    i = (zz * 2 + bb) * fr
                    g[m, j, bb, zz] = out[i:i + fr]
            return carry

        lax.fori_loop(0, blocks, one, 0)

    feed_grad(0, gb[...], hid)
    down_sum.core()

    load_out = []

    def feed_back(i, carry):
        at = pl.ds(pl.multiple_of(i * padded, padded), padded)
        low = gb[at, :]
        acc = g2[at, :]
        for j in range(blocks):
            gp = (slope[j, at, :].astype(F32) * mm(low, wb[1, j], 1, 1)).astype(BF16)
            slope[j, at, :] = gp
            bv[UP + j:UP + j + 1, :] += col_sum(gp.astype(F32))
            acc = acc + mm(gp, wb[0, j])
        nn = en[at, :]
        bv[GAIN1:GAIN1 + 1, :] += col_sum(acc * nn)
        bv[SHIFT1:SHIFT1 + 1, :] += col_sum(acc)
        gg = acc * vec[GAIN1:GAIN1 + 1, :]
        inv = inv1[at, 0:1]
        back = inv * (gg - row_mean(gg) - nn * row_mean(gg * nn))
        g2[at, :] = back
        ga = back.astype(BF16)
        flow2 = ga
        bv[OUT:OUT + 1, :] += col_sum(ga.astype(F32))
        gm = mm(ga, wo[...], 1, 1)
        gb[at, :] = (gm * rinv[at, :].astype(F32)).astype(BF16)
        hid[0, at, :] = flow2
        return carry

    lax.fori_loop(0, blocks, feed_back, 0)
    down_sum.first()
    feed_grad(1, flow[...], slope)
    up_sum.core()

    out_sum = MatrixSum(go, rco, r1o, r2o, rzo, o_out, True)
    out_grad = mm(mx[...], hid[0], 0, 0).astype(BF16)
    for i in range(8):
        r = width // 8
        go[i // 4, (i // 2) % 2, i % 2] = out_grad[i * r:(i + 1) * r]
    out_steps = out_sum.steps()
    next(out_steps)

    tile_b = n // 2
    zs = rzo.shape[0]
    pair_sums = []

    def attend_back(p):
        lanes = pl.ds(p * 128, 128)
        qt[...] = qkv[p, :, 0:128].T
        dt[...] = gb[:, lanes].T
        for h in range(2):
            def tile(i, carry):
                at = pl.ds(pl.multiple_of(i * tile_b, tile_b), tile_b)
                d = gb[at, lanes]
                own = (lane // 64) == h
                dm = jnp.where(own, d, jnp.zeros_like(d))
                centre = jnp.sum(
                    jnp.where(own, d.astype(F32) * mxf[at, lanes], 0.0), axis=1, keepdims=True
                )
                s = (mm(dm, qkv[p, :, 256:384], 1, 1) - centre).astype(BF16)
                s = s * prob[2 * p + h, at, :]
                ds[at, :] = s
                dq = mm(s, qkv[p, :, 128:256])
                if h == 0:
                    mxf[at, lanes] = jnp.where(lane < 64, dq, mxf[at, lanes])
                else:
                    dq = jnp.where(lane < 64, mxf[at, lanes], dq) * 0.125
                    rinv[at, lanes] = dq.astype(BF16)
                return carry

            lax.fori_loop(0, n // tile_b, tile, 0, unroll=True)
            half = slice(64 * h, 64 * h + 64)
            dk = mm(qt[half, :], ds[...])
            dv = mm(dt[half, :], prob[2 * p + h])
            qt[half, :] = dk.astype(BF16)
            dt[half, :] = dv.astype(BF16)
        dq = rinv[:, lanes]
        dv = dt[...].T
        qkv[p, :, 0:128] = dq
        qkv[p, :, 128:256] = qt[...].T
        qkv[p, :, 256:384] = dv
        bv[QUERY:QUERY + 1, lanes] += col_sum(dq.astype(F32))
        bv[VALUE:VALUE + 1, lanes] += col_sum(dv.astype(F32))
        grads = qkv[p, :, 0:384]
        grad = mm(elow[...], grads, 0, 0).astype(BF16)
        for i in range(8):
            r = width // 8
            gq[p, i // 4, (i // 2) % 2, i % 2] = grad[i * r:(i + 1) * r]
        one = MatrixSum(
            gq.at[p], rcq.at[p], r1q.at[p], r2q.at[p], rzq.at[p], o_qkv.at[p], p % 2 == 1
        )
        steps = one.steps()
        next(steps)
        pair_sums.append(steps)
        g2[...] += mm(grads, wqkv[p], 1, 1)

    def advance(steps):
        next(steps, None)

    attend_back(0)
    down_sum.second()
    up_sum.first()
    advance(out_steps)
    attend_back(1)
    down_sum.third()
    up_sum.second()
    advance(out_steps)
    advance(pair_sums[0])
    attend_back(2)
    down_sum.last()
    up_sum.third()
    advance(out_steps)
    advance(pair_sums[0])
    advance(pair_sums[1])
    attend_back(3)
    up_sum.last()
    advance(out_steps)
    for i in (0, 1, 2):
        advance(pair_sums[i])

    low = g2[...].astype(BF16)
    bv[EMBED:EMBED + 1, :] += col_sum(low.astype(F32))
    grad = mm(xp[...], low, 0, 0)
    look = grad.shape[0]
    whole = jnp.concatenate(
        [grad, bv[0:UP + blocks, :], jnp.zeros((128 - look - UP - blocks, width), F32)], axis=0
    ).astype(BF16)
    for i in range(8):
        tb[i] = whole[16 * i:16 * i + 16]
    me = c * 4 + y * 2 + b
    tail = []
    for k, (pc, py, pb) in enumerate(peers):
        cp = sems.copy(tb.at[pc * 4 + py * 2 + pb], rt.at[k], dev(pc, py, pb))
        cp.start()
        tail.append(cp)
    out = mm(low, we[...], 1, 1)
    for i in range(blocks):
        xs[i] = out[i * padded:i * padded + rows].astype(BF16)
    own_s = sems.local(xs.at[t], o_series.at[t])
    own_s.start()
    send_s = exchange(xs, o_series)
    for cp in send_s:
        cp.start()
    advance(out_steps)
    for i in (0, 1, 2, 3):
        advance(pair_sums[i])
    for cp in tail:
        cp.wait()
    total = tb[me].astype(F32)
    for k in range(7):
        total = total + rt[k].astype(F32)
    tb[me] = total.astype(BF16)
    tail = []
    rtz[z] = tb[me]
    for k in range(1, nz):
        cp = sems.copy(tb.at[me], rtz.at[z], dev(c, y, b, (z + k) % nz))
        cp.start()
        tail.append(cp)
    for i in (0, 1, 2, 3):
        advance(pair_sums[i])
    advance(out_steps)
    for cp in tail:
        cp.wait()
    total = rtz[0].astype(F32)
    for k in range(1, nz):
        total = total + rtz[k].astype(F32)
    o_tail[me] = total.astype(BF16)
    tail = []
    for pc, py, pb in peers:
        cp = sems.copy(o_tail.at[me], o_tail.at[me], dev(pc, py, pb))
        cp.start()
        tail.append(cp)
    for _ in range(8 + zs):
        advance(out_steps)
        for i in (0, 1, 2, 3):
            advance(pair_sums[i])
    for cp in tail + send_s + send_mixed:
        cp.wait()
    own_s.wait()
    own_mixed.wait()


def body(
    series, embed_weight, embed_bias, query_weight, query_bias, key_weight, value_weight,
    value_bias, out_weight, out_bias, first_gain, first_shift, up_weight, up_bias,
    down_weight, down_bias, second_gain, second_shift, cotangent,
    *, dp_size, tensor_size,
):
    windows, rows, look = series.shape
    width = embed_weight.shape[1]
    hidden = up_weight.shape[0]
    pairs = HEADS // 2
    assert windows == tensor_size == 4 and width == HEADS * 64 and dp_size % 2 == 0
    padded = -(-rows // 32) * 32
    n = tensor_size * padded
    nz = dp_size // 2
    fr = width // dp_size
    r = width // 8
    zs = nz if nz <= DIRECT else doublings(nz)

    vec = jnp.stack([
        embed_bias, query_bias, value_bias, out_bias, first_gain, first_shift, down_bias,
        second_gain, second_shift,
    ])
    vec = jnp.pad(vec, ((0, 16 - vec.shape[0]), (0, 0)))
    ub = jnp.broadcast_to(up_bias.astype(F32)[None, :], (8, hidden))

    def scr(*shape, dtype=BF16):
        return pltpu.VMEM(shape, dtype)

    scratch = [
        scr(4, rows, look),
        scr(n, look),
        scr(n, width, dtype=F32),
        scr(n, width),
        scr(pairs, n, 512),
        scr(HEADS, n, n),
        scr(n, n),
        scr(n, width, dtype=F32),
        scr(n, width),
        scr(n, width),
        scr(n, 128, dtype=F32),
        scr(n, width),
        scr(4, n, hidden),
        scr(4, n, hidden),
        scr(4, rows, width),
        scr(n, width, dtype=F32),
        scr(n, width),
        scr(128, n),
        scr(128, n),
        scr(2, 4, hidden, width),
        scr(pairs, width, 384),
        scr(width, width),
        scr(look, width),
        scr(4, 8, hidden, dtype=F32),
        scr(2, 4, 2, nz, fr, hidden),
        scr(2, 2, 2, nz, fr, hidden),
        scr(2, 2, nz, fr, hidden),
        scr(2, nz, fr, hidden),
        scr(2, nz - 1, fr, hidden),
        scr(pairs, 2, 2, 2, r, 384),
        scr(pairs, 2, 2, r, 384),
        scr(pairs, 2, r, 384),
        scr(pairs, r, 384),
        scr(pairs, zs, r, 384),
        scr(2, 2, 2, r, width),
        scr(2, 2, r, width),
        scr(2, r, width),
        scr(r, width),
        scr(zs, r, width),
        scr(8, 16, width),
        scr(7, 16, width),
        scr(nz, 16, width),
        scr(16, width, dtype=F32),
        pltpu.SemaphoreType.DMA((N_SEMS + 16 * nz,)),
        pltpu.SemaphoreType.DMA((N_SEMS + 16 * nz,)),
    ]
    hbm = pl.BlockSpec(memory_space=pl.ANY)
    vmem = pl.BlockSpec(memory_space=pltpu.VMEM)
    sd = jax.ShapeDtypeStruct
    mixed, sgrad, g_qkv, g_out, g_up, g_down, tail = pl.pallas_call(
        functools.partial(kernel, (4, rows, padded, nz, fr)),
        out_shape=[
            sd((4, rows, width), BF16),
            sd((4, rows, look), BF16),
            sd((pairs, 2, 2, 2, r, 384), BF16),
            sd((2, 2, 2, r, width), BF16),
            sd((fr, hidden), F32),
            sd((fr, hidden), F32),
            sd((8, 16, width), BF16),
        ],
        in_specs=[hbm] * 9 + [vmem] * 2,
        out_specs=[hbm] * 2 + [vmem] * 5,
        scratch_shapes=scratch,
        compiler_params=pltpu.CompilerParams(
            collective_id=1, has_side_effects=True, vmem_limit_bytes=64 * 1024 * 1024
        ),
    )(
        series, cotangent, embed_weight, query_weight, key_weight, value_weight, out_weight,
        up_weight, down_weight, vec, ub,
    )
    g_qkv = g_qkv.reshape(pairs, width, 3, 128).astype(F32)
    g_qkv = g_qkv.transpose(2, 1, 0, 3).reshape(3, width, width)
    tail = tail.reshape(128, width).astype(F32)
    vecs = tail[look:look + UP + 4]
    return (
        mixed,
        sgrad,
        tail[:look],
        vecs[EMBED],
        g_qkv[0],
        vecs[QUERY],
        g_qkv[1],
        g_qkv[2],
        vecs[VALUE],
        g_out.reshape(width, width).astype(F32),
        vecs[OUT],
        vecs[GAIN1],
        vecs[SHIFT1],
        g_up.T,
        vecs[UP:UP + 4].reshape(4 * hidden),
        g_down.T,
        vecs[DOWN],
        vecs[GAIN2],
        vecs[SHIFT2],
    )


def solution(mesh):
    token = P("dp", "tensor", None)
    return jax.shard_map(
        functools.partial(
            body, dp_size=mesh.shape["dp"], tensor_size=mesh.shape["tensor"]
        ),
        mesh=mesh,
        in_specs=(
            token, P(), P(), P(), P(), P(), P(), P(), P(), P(), P(), P(),
            P("tensor", None), P("tensor"), P("tensor", None), P(), P(), P(), token,
        ),
        out_specs=(
            token, token, P(), P(), P(), P(), P(), P(), P(), P(), P(), P(), P(),
            P("tensor", "dp"), P(), P("tensor", "dp"), P(), P(), P(),
        ),
        check_vma=False,
    )
```

```python
import functools
import jax
import jax.numpy as jnp
from jax import lax
from jax.experimental import pallas as pl
from jax.experimental.pallas import tpu as pltpu
from jax.sharding import PartitionSpec as P

HEADS = 8
EPSILON = 1e-05
F32 = jnp.float32
BF16 = jnp.bfloat16
MESH = pl.DeviceIdType.MESH
GELU_A = 0.7978845608028654
GELU_B = GELU_A * 0.044715
MASKED = -1e30

EMBED, QUERY, VALUE, OUT, GAIN1, SHIFT1, DOWN, GAIN2, SHIFT2 = range(9)
S_GAIN1, S_SHIFT1, S_DOWN, S_GAIN2, S_SHIFT2, S_UP = range(1, 7)


def mm(left, right, cl=1, cr=0):
    return lax.dot_general(
        left, right, (((cl,), (cr,)), ((), ())), preferred_element_type=F32
    )


def row_mean(x):
    return jnp.mean(x, axis=1, keepdims=True)


def col_sum(x):
    return jnp.sum(x, axis=0, keepdims=True)


def pad_rows(x, rows):
    if x.shape[0] == rows:
        return x
    return jnp.concatenate([x, jnp.zeros((rows - x.shape[0], x.shape[1]), x.dtype)], axis=0)


class Sems:
    def __init__(self, send, recv):
        self.send, self.recv, self.used = send, recv, 0

    def copy(self, src, dst, device):
        i = self.used
        self.used += 1
        return pltpu.make_async_remote_copy(
            src_ref=src,
            dst_ref=dst,
            send_sem=self.send.at[i],
            recv_sem=self.recv.at[i],
            device_id=device,
            device_id_type=MESH,
        )

    def local(self, src, dst):
        i = self.used
        self.used += 1
        return pltpu.make_async_copy(src, dst, self.send.at[i])

    def slot(self):
        i = self.used
        self.used += 1
        return self.send.at[i], self.recv.at[i]


N_SEMS = 192


def kernel(
    cfg,
    series, cot_in, w_embed, w_q, w_k, w_v, w_o, w_up, w_down,
    b_embed, b_query, b_value, b_out, gain1, shift1, b_down, gain2, shift2, b_up,
    o_mixed, o_series, o_pairs, o_out, o_small, o_up, o_down,
    xs, xa, en, qkv, prob, ds, mxf, mx, rinv, inv1, flow, hid, slope, cot, g2, gb,
    qt, dt, wb, wqkv, wo, we, w2, ubb,
    g, rc, r1y, r1x, r2, rz,
    gp_, gprc, gpr1, gprz,
    go, gorc, gor1, gorz,
    gs, gsrc, gsr1, gsrz,
    vec, ubl, send, recv,
):
    blocks, rows, padded, nz, fr = cfg
    n = blocks * padded
    look = we.shape[0]
    width = wo.shape[0]
    pairs = qkv.shape[0]
    hidden = w_up.shape[0]
    lanes2 = hidden // 2
    dp, t = lax.axis_index("dp"), lax.axis_index("tensor")
    c, y = t % 2, t // 2
    b, z = dp % 2, dp // 2
    co, yo, bo = 1 - c, 1 - y, 1 - b
    xy = y * 2 + b
    sems = Sems(send, recv)

    def dev(cc, yy, bb, zz=None):
        return ((z if zz is None else zz) * 2 + bb, yy * 2 + cc)

    core_dev, y_dev, x_dev = dev(co, y, b), dev(c, yo, b), dev(c, y, bo)
    xy_peers = [(y, bo), (yo, b), (yo, bo)]

    barrier = pltpu.get_barrier_semaphore()
    partners = [dev(co, y, b), dev(co, yo, b)]
    partners += [dev(c, py, pb) for py, pb in xy_peers]
    partners += [dev(c, y, b, (z + k) % nz) for k in range(1, nz)]
    for partner in partners:
        pl.semaphore_signal(barrier, inc=1, device_id=partner, device_id_type=MESH)

    def load(src, dst):
        cp = sems.local(src, dst)
        cp.start()
        return cp

    load_we = load(w_embed, we)
    load_qkv = []
    for p in range(pairs):
        for j, w in enumerate((w_q, w_k, w_v)):
            load_qkv.append(load(
                w.at[:, 128 * p:128 * p + 128], wqkv.at[p, :, 128 * j:128 * j + 128]
            ))
    own_x = load(series.at[t], xs.at[t, 0:look])
    own_w = [load(w, wb.at[m, t]) for m, w in enumerate((w_up, w_down))]
    load_wo = load(w_o, wo)
    own_cot = load(cot_in.at[t], cot.at[t])
    for i, ref in enumerate(
        (b_embed, b_query, b_value, b_out, gain1, shift1, b_down, gain2, shift2)
    ):
        vec[i:i + 1, :] = ref[...]
    ubl[...] = jnp.broadcast_to(b_up[...].astype(F32), ubl.shape)
    ubb[t] = ubl[...]
    tail_rows = xs.shape[1] - look
    first = lax.broadcasted_iota(jnp.int32, (tail_rows, rows), 0) == 0
    for i in range(blocks):
        xs[i, look:, :] = jnp.where(first, 1.0, 0.0).astype(BF16)

    pl.semaphore_wait(barrier, len(partners))

    def exchange(src, dst, dst_at):
        out = []
        for k in range(1, blocks):
            other = (t + k) % blocks
            out.append(sems.copy(src.at[other], dst_at(dst), (dp, other)))
        return out

    send_x = exchange(series, xs, lambda r: r.at[t, 0:look])
    part = hidden // 4
    t_y, t_c, t_d = yo * 2 + c, y * 2 + co, yo * 2 + co
    stage_y, stage_core, stage_ub, stage_x, stage_d, stage_e = [], [], [], [], [], []
    for s in range(2):
        at = pl.ds(pl.multiple_of((b * 2 + s) * part, part), part)
        far = pl.ds(pl.multiple_of((bo * 2 + s) * part, part), part)
        for m, w in enumerate((w_up, w_down)):
            stage_y.append(sems.copy(w.at[at], wb.at[m, t, at], y_dev))
            stage_x.append(sems.copy(wb.at[m, t_y, at], wb.at[m, t_y, at], x_dev))
            stage_d.append(sems.copy(wb.at[m, t_y, at], wb.at[m, t_y, at], core_dev))
            stage_e.append(sems.copy(wb.at[m, t_y, far], wb.at[m, t_y, far], core_dev))
    for m, w in enumerate((w_up, w_down)):
        stage_core.append(sems.copy(w, wb.at[m, t], core_dev))
    for k in range(1, blocks):
        other = (t + k) % blocks
        stage_ub.append(sems.copy(ubl, ubb.at[t], (dp, other)))
    send_cot = exchange(cot_in, cot, lambda r: r.at[t])
    for cp in send_x + stage_ub + stage_y + stage_core + send_cot:
        cp.start()

    def forward_y(i):
        stage_y[i].wait_recv()
        stage_x[i].start()
        stage_d[i].start()

    def forward_x(i):
        stage_x[i].wait_recv()
        stage_e[i].start()

    load_we.wait()
    one_row = lax.broadcasted_iota(jnp.int32, (128, 1), 0)
    b_high = vec[EMBED:EMBED + 1, :].astype(BF16)
    b_low = vec[EMBED:EMBED + 1, :] - b_high.astype(F32)
    we_rows = pad_rows(we[...].astype(F32), 128)
    high = we_rows + jnp.where(one_row == look, b_high.astype(F32), 0.0)
    low = jnp.where(one_row == look, b_low, 0.0)
    w2[0, 0:128, :] = high.astype(BF16)
    w2[0, 128:256, :] = low.astype(BF16)
    both = (high + jnp.where(one_row == look + 1, b_low, 0.0)).astype(BF16)
    for cp in load_qkv:
        cp.wait()
    for p in range(pairs):
        at = slice(128 * p, 128 * p + 128)
        prod = mm(both, wqkv[p])
        bias = prod[look:look + 1] + prod[look + 1:look + 2]
        bias = bias + jnp.concatenate(
            [vec[QUERY:QUERY + 1, at], jnp.zeros((1, 128), F32), vec[VALUE:VALUE + 1, at]],
            axis=1,
        )
        prod = jnp.where(one_row < look, prod, jnp.where(one_row == look, bias, 0.0))
        factor = lax.broadcasted_iota(jnp.int32, (1, 384), 1)
        prod = prod * jnp.where(factor < 128, 0.125, 1.0)
        high = prod.astype(BF16)
        w2[1 + p, 0:128, 0:384] = high
        w2[1 + p, 128:256, 0:384] = (prod - high.astype(F32)).astype(BF16)
        qkv[p, :, 384:512] = jnp.ones((n, 128), BF16)

    own_x.wait()
    for cp in send_x:
        cp.wait()
    for i in range(blocks):
        x = pad_rows(xs[i].astype(F32).T, padded).astype(BF16)
        at = pl.ds(i * padded, padded)
        xa[at, 0:128] = x
        xa[at, 128:256] = x
    en[...] = mm(xa[...], w2[0])

    def project(p, carry):
        qkv[p, :, 0:384] = mm(xa[...], w2[1 + p, :, 0:384]).astype(BF16)
        return carry

    lax.fori_loop(0, pairs, project, 0)

    lane = lax.broadcasted_iota(jnp.int32, (1, 128), 1)
    key_at = lax.broadcasted_iota(jnp.int32, (1, n), 1)
    mask = jnp.where(key_at % padded >= rows, MASKED, 0.0).astype(F32)

    tile_f = 128

    def attend_pair(p, carry):
        for k, do in enumerate(((forward_y, 0), (forward_y, 1), (forward_y, 2), (forward_y, 3))):
            pl.when(p == k)(functools.partial(*do))
        pl.when(p == 3)(functools.partial(forward_x, 0))

        def attend_tile(i, carry):
            at = pl.ds(pl.multiple_of(i * tile_f, tile_f), tile_f)
            q = qkv[p, at, 0:128]
            outs, inverses = [], []
            for h in range(2):
                qm = jnp.where((lane // 64) == h, q, jnp.zeros_like(q))
                s = mm(qm, qkv[p, :, 128:256], 1, 1) + mask
                e = jnp.exp(s - jnp.max(s, axis=1, keepdims=True)).astype(BF16)
                prob[2 * p + h, at, :] = e
                o = mm(e, qkv[p, :, 256:512])
                outs.append(o[:, :128])
                inverses.append(1.0 / o[:, 128:])
            inverse = jnp.where(lane < 64, inverses[0], inverses[1])
            o = jnp.where(lane < 64, outs[0], outs[1]) * inverse
            lanes = pl.ds(pl.multiple_of(p * 128, 128), 128)
            mxf[at, lanes] = o
            mx[at, lanes] = o.astype(BF16)
            rinv[at, lanes] = inverse.astype(BF16)
            return carry

        lax.fori_loop(0, n // tile_f, attend_tile, 0, unroll=True)
        return carry

    lax.fori_loop(0, pairs, attend_pair, 0)
    forward_x(1)
    forward_x(2)

    load_wo.wait()

    def first_norm(i, carry):
        at = pl.ds(pl.multiple_of(i * padded, padded), padded)
        zz = en[at, :] + (mm(mx[at, :], wo[...]) + vec[OUT:OUT + 1, :])
        centred = zz - row_mean(zz)
        inv = lax.rsqrt(row_mean(centred * centred) + EPSILON)
        nn = centred * inv
        en[at, :] = nn
        inv1[at, :] = jnp.broadcast_to(inv, (padded, 128))
        out = nn * vec[GAIN1:GAIN1 + 1, :] + vec[SHIFT1:SHIFT1 + 1, :]
        flow[at, :] = out.astype(BF16)
        g2[at, :] = out + vec[DOWN:DOWN + 1, :]
        return carry

    lax.fori_loop(0, blocks, first_norm, 0)
    forward_x(3)

    tile_h = n // 2

    def feed_forward(j):
        for i in range(n // tile_h):
            at = slice(i * tile_h, (i + 1) * tile_h)
            v = mm(flow[at, :], wb[0, j], 1, 1) + ubb[j, 0:1, :]
            v2 = v * v
            half = 0.5 * jnp.tanh(v * (GELU_A + GELU_B * v2)) + 0.5
            h = v * half
            slope[j, at, :] = (
                half + h * (1.0 - half) * (2 * GELU_A + (6 * GELU_B) * v2)
            ).astype(BF16)
            h = h.astype(BF16)
            hid[j, at, :] = h
            g2[at, :] += mm(h, wb[1, j])

    for cp in own_w:
        cp.wait()
    feed_forward(t)
    for cp in stage_core + stage_ub:
        cp.wait()
    feed_forward(t_c)
    for cp in stage_x + stage_y:
        cp.wait_send()
    feed_forward(t_y)
    for cp in stage_d + stage_e:
        cp.wait()
    feed_forward(t_d)

    own_cot.wait()
    for cp in send_cot:
        cp.wait()

    def add_row(row, value, at=slice(None)):
        i = look + row
        gs[i // 64, (i // 16) % 4, i % 16:i % 16 + 1, at] += value

    gs[...] = jnp.zeros_like(gs)

    def second_norm(i, carry):
        at = pl.ds(pl.multiple_of(i * padded, padded), padded)
        acc = g2[at, :]
        centred = acc - row_mean(acc)
        inv = lax.rsqrt(row_mean(centred * centred) + EPSILON)
        nn = centred * inv
        up = pad_rows(cot[i].astype(F32), padded)
        result = nn * vec[GAIN2:GAIN2 + 1, :] + vec[SHIFT2:SHIFT2 + 1, :]
        cot[i] = result[:rows].astype(BF16)
        gg = up * vec[GAIN2:GAIN2 + 1, :]
        back = inv * (gg - row_mean(gg) - nn * row_mean(gg * nn))
        g2[at, :] = back
        low = back.astype(BF16)
        gb[at, :] = low
        add_row(S_GAIN2, col_sum(up * nn))
        add_row(S_SHIFT2, col_sum(up))
        add_row(S_DOWN, col_sum(low.astype(F32)))
        return carry

    lax.fori_loop(0, blocks, second_norm, 0)
    own_mixed = sems.local(cot.at[t], o_mixed.at[t])
    own_mixed.start()
    send_mixed = exchange(cot, o_mixed, lambda r: r.at[t])

    def add_into(dst, src, index):
        dst[index] = (dst[index].astype(F32) + src[...].astype(F32)).astype(dst.dtype)

    class FeedSum:
        def __init__(self, m, out):
            self.m, self.out = m, out
            self.flight = {}

        def start(self, key, src, dst, device):
            cp = sems.copy(src, dst, device)
            cp.start()
            self.flight.setdefault(key, []).append(cp)

        def wait(self, key):
            for cp in self.flight.pop(key):
                cp.wait()

        def ready(self, k):
            m = self.m
            if k < 2:
                self.start(("core", k), g.at[m, k], rc.at[m, k], core_dev)
                return
            self.wait(("core", k - 2))
            for h in range(2):
                for bb in range(2):
                    for zz in range(nz):
                        add_into(g, rc.at[m, k - 2, h, bb, zz], (m, k, h, bb, zz))
            if k == 2:
                self.start("y0", g.at[m, 2, 0], r1y.at[m], y_dev)
            self.start("x1", g.at[m, k, 1, bo], r1x.at[m, k - 2], x_dev)

        def second(self, h):
            m = self.m
            if h == 0:
                self.wait("y0")
                for bb in range(2):
                    for zz in range(nz):
                        add_into(g, r1y.at[m, bb, zz], (m, 3, 0, bb, zz))
                self.start("x0", g.at[m, 3, 0, bo], r2.at[m, 0], x_dev)
            else:
                self.wait("x1")
                for k in range(2):
                    for zz in range(nz):
                        add_into(g, r1x.at[m, k, zz], (m, 2 + k, 1, b, zz))
                self.start("y1", g.at[m, 2, 1, b], r2.at[m, 1], y_dev)

        def third(self, h):
            m = self.m
            self.wait("x0" if h == 0 else "y1")
            for zz in range(nz):
                add_into(g, r2.at[m, h, zz], (m, 3, h, b, zz))
            for k in range(1, nz):
                zz = (z + k) % nz
                self.start(
                    ("z", h), g.at[m, 3, h, b, zz], rz.at[m, h, k - 1], dev(c, y, b, zz)
                )

        def last(self, h):
            m = self.m
            self.wait(("z", h))
            total = g[m, 3, h, b, z].astype(F32)
            for k in range(nz - 1):
                total = total + rz[m, h, k].astype(F32)
            self.out[:, h * lanes2:(h + 1) * lanes2] = total

    class WholeSum:
        def __init__(self, grad, rcv, rcv1, rcvz, out):
            self.refs = (grad, rcv, rcv1, rcvz, out)

        def start(self, src, dst, device):
            cp = sems.copy(src, dst, device)
            cp.start()
            self.cps.append(cp)

        def wait(self):
            for cp in self.cps:
                cp.wait()
            self.cps = []

        def steps(self):
            grad, rcv, rcv1, rcvz, out = self.refs
            self.cps = []
            self.start(grad.at[co], rcv, core_dev)
            yield
            self.wait()
            for i in range(4):
                add_into(grad, rcv.at[i], (c, i))
            for k, (py, pb) in enumerate(xy_peers):
                self.start(grad.at[c, py * 2 + pb], rcv1.at[k], dev(c, py, pb))
            yield
            self.wait()
            total = grad[c, xy].astype(F32)
            for k in range(3):
                total = total + rcv1[k].astype(F32)
            rcvz[z] = total.astype(grad.dtype)
            for k in range(1, nz):
                self.start(rcvz.at[z], rcvz.at[z], dev(c, y, b, (z + k) % nz))
            yield
            self.wait()
            total = rcvz[0].astype(F32)
            for k in range(1, nz):
                total = total + rcvz[k].astype(F32)
            out[c, xy] = total.astype(grad.dtype)
            for py, pb in xy_peers:
                self.start(out.at[c, xy], out.at[c, xy], dev(c, py, pb))
            yield
            self.wait()
            self.start(out.at[c], out.at[c], core_dev)
            yield
            self.wait()

    down_sum, up_sum = FeedSum(0, o_down), FeedSum(1, o_up)
    order = (t_d, t_c, t_y, t)

    def feed_grad(m, k, left, right):
        out = mm(left, right, 0, 0).astype(BF16)
        for h in range(2):
            for zz in range(nz):
                for bb in range(2):
                    i = (zz * 2 + bb) * fr
                    g[m, k, h, bb, zz] = out[i:i + fr, h * lanes2:(h + 1) * lanes2]

    for k, j in enumerate(order):
        feed_grad(0, k, gb[...], hid[j])
        down_sum.ready(k)
    for cp in send_mixed[:2]:
        cp.start()

    def feed_back(k, j):
        for i in range(n // tile_h):
            at = slice(i * tile_h, (i + 1) * tile_h)
            gp = (slope[j, at, :].astype(F32) * mm(gb[at, :], wb[1, j], 1, 1)).astype(BF16)
            slope[j, at, :] = gp
            g2[at, :] += mm(gp, wb[0, j])
        up_rows[k] = col_sum(slope[j].astype(F32))
        feed_grad(1, k, flow[...], slope[j])

    up_rows = [None] * blocks
    for k, j in enumerate(order):
        feed_back(k, j)
        up_sum.ready(k)
        if k == 1:
            down_sum.second(0)
            down_sum.second(1)
        if k == 3:
            down_sum.third(0)
            down_sum.third(1)
    for k, j in enumerate(order):
        i = look + S_UP + j
        gs[i // 64, (i // 16) % 4, pl.ds(i % 16, 1), :] = up_rows[k]
    for cp in send_mixed[2:]:
        cp.start()

    def first_back(i, carry):
        at = pl.ds(pl.multiple_of(i * padded, padded), padded)
        acc = g2[at, :]
        nn = en[at, :]
        add_row(S_GAIN1, col_sum(acc * nn))
        add_row(S_SHIFT1, col_sum(acc))
        gg = acc * vec[GAIN1:GAIN1 + 1, :]
        inv = inv1[at, 0:1]
        back = inv * (gg - row_mean(gg) - nn * row_mean(gg * nn))
        ga = back.astype(BF16)
        hid[0, at, :] = ga
        gm = mm(ga, wo[...], 1, 1)
        gb[at, :] = (gm * rinv[at, :].astype(F32)).astype(BF16)
        return carry

    lax.fori_loop(0, blocks, first_back, 0)

    ga = hid.at[0]
    out_grad = mm(mx[...], ga[...], 0, 0).astype(BF16)
    for i in range(8):
        r = width // 8
        go[i // 4, i % 4] = out_grad[i * r:(i + 1) * r]
    out_steps = WholeSum(go, gorc, gor1, gorz, o_out).steps()
    next(out_steps)
    small = mm(xa[:, 0:128], ga[...], 0, 0)
    for i in range(8):
        gs[i // 4, i % 4] += small[16 * i:16 * i + 16]
    small_steps = WholeSum(gs, gsrc, gsr1, gsrz, o_small).steps()
    next(small_steps)

    tile_b = n // 2
    pair_steps = []

    def attend_back(p, between):
        lanes = pl.ds(p * 128, 128)
        qt[...] = qkv[p, :, 0:128].T
        dt[...] = gb[:, lanes].T
        for h in range(2):
            def tile(i, carry):
                at = pl.ds(pl.multiple_of(i * tile_b, tile_b), tile_b)
                d = gb[at, lanes]
                own = (lane // 64) == h
                dm = jnp.where(own, d, jnp.zeros_like(d))
                centre = jnp.sum(
                    jnp.where(own, d.astype(F32) * mxf[at, lanes], 0.0), axis=1, keepdims=True
                )
                s = (mm(dm, qkv[p, :, 256:384], 1, 1) - centre).astype(BF16)
                s = s * prob[2 * p + h, at, :]
                ds[at, :] = s
                dq = mm(s, qkv[p, :, 128:256])
                if h == 0:
                    mxf[at, lanes] = jnp.where(lane < 64, dq, mxf[at, lanes])
                else:
                    rinv[at, lanes] = jnp.where(lane < 64, mxf[at, lanes], dq).astype(BF16)
                return carry

            lax.fori_loop(0, n // tile_b, tile, 0, unroll=True)
            half = slice(64 * h, 64 * h + 64)
            dk = mm(qt[half, :], ds[...])
            dv = mm(dt[half, :], prob[2 * p + h])
            qt[half, :] = dk.astype(BF16)
            dt[half, :] = dv.astype(BF16)
            between[h]()
        qkv[p, :, 0:128] = rinv[:, lanes]
        qkv[p, :, 128:256] = qt[...].T
        qkv[p, :, 256:384] = dt[...].T
        grad = mm(xa[:, 0:128], qkv[p, :, 0:384], 0, 0).astype(BF16)
        for i in range(8):
            gp_[p, i // 4, i % 4] = grad[16 * i:16 * i + 16]
        steps = WholeSum(
            gp_.at[p], gprc.at[p], gpr1.at[p], gprz.at[p], o_pairs.at[p]
        ).steps()
        next(steps)
        pair_steps.append(steps)

    def advance(*steps):
        for s in steps:
            next(s, None)

    def at_0a():
        down_sum.last(0)
        down_sum.last(1)

    def at_0b():
        up_sum.second(0)
        up_sum.second(1)
        advance(out_steps, small_steps)

    def at_1a():
        pass

    def at_1b():
        up_sum.third(0)
        up_sum.third(1)
        advance(out_steps, small_steps, pair_steps[0])

    def at_2a():
        pass

    def at_2b():
        advance(out_steps, small_steps, pair_steps[0], pair_steps[1])

    def at_3a():
        advance(pair_steps[0])

    def at_3b():
        up_sum.last(0)
        up_sum.last(1)
        advance(out_steps, small_steps, pair_steps[1], pair_steps[2])

    attend_back(0, (at_0a, at_0b))
    attend_back(1, (at_1a, at_1b))
    attend_back(2, (at_2a, at_2b))
    attend_back(3, (at_3a, at_3b))

    out = mm(we[...], ga[...], 1, 1)
    for p in range(pairs):
        out = out + mm(w2[1 + p, 0:look, 0:384], qkv[p, :, 0:384], 1, 1)
    for i in range(blocks):
        xs[i, 0:look, :] = out[:, i * padded:i * padded + rows].astype(BF16)
    own_s = sems.local(xs.at[t, 0:look], o_series.at[t])
    own_s.start()
    send_s = []
    for k in range(1, blocks):
        other = (t + k) % blocks
        send_s.append(sems.copy(xs.at[other, 0:look], o_series.at[t], (dp, other)))
    for cp in send_s:
        cp.start()
    for _ in range(5):
        advance(*pair_steps, out_steps, small_steps)
    for cp in send_s + send_mixed:
        cp.wait()
    own_s.wait()
    own_mixed.wait()


def finish(cfg, *refs):
    pairs, n_in, n_out = cfg
    inputs, refs = refs[:n_in], refs[n_in:]
    results, refs = refs[:n_out], refs[n_out:]
    held, refs = refs[:n_in], refs[n_in:]
    made, (sem_in, sem_out) = refs[:-2], refs[-2:]
    mixed, sgrad, up, down, pair_sums, out, small, we, wq, wk, wv, be = held
    made = (mixed, sgrad, up, down) + tuple(made)
    loads = [
        pltpu.make_async_copy(src, dst, sem_in.at[i])
        for i, (src, dst) in enumerate(zip(inputs, held))
    ]
    stores = [
        pltpu.make_async_copy(src, dst, sem_out.at[i])
        for i, (src, dst) in enumerate(zip(made, results))
    ]
    o_q, o_k, o_v, o_o, o_we, o_be, o_bq, o_bv, o_bo, o_g1, o_s1, o_bu, o_bd, o_g2, o_s2 = made[4:]
    for i in (4, 7, 11, 8, 9, 10, 6, 5, 0, 1, 2, 3):
        loads[i].start()
    look, width = we.shape
    r = width // 8
    for i in (4, 7, 11):
        loads[i].wait()
    row = lax.broadcasted_iota(jnp.int32, (128, 1), 0)
    b_high = be[...].astype(BF16).astype(F32)
    left = pad_rows(we[...].astype(F32), 128)
    left = left + jnp.where(row == look, b_high, 0.0)
    left = (left + jnp.where(row == look + 1, be[...] - b_high, 0.0)).astype(BF16)
    total = jnp.zeros((128, width), F32)
    for j, (o, w) in enumerate(((o_q, wq), (o_k, wk), (o_v, wv))):
        sums = jnp.concatenate(
            [
                jnp.concatenate(
                    [pair_sums[p, i // 4, i % 4, :, 128 * j:128 * j + 128] for i in range(8)],
                    axis=0,
                ).astype(F32)
                for p in range(pairs)
            ],
            axis=1,
        )
        if j == 0:
            sums = sums * 0.125
        last = sums[look:look + 1]
        o[...] = mm(left, (sums + jnp.where(row == look + 1, last, 0.0)).astype(BF16), 0, 0)
        stores[4 + j].start()
        if j == 0:
            o_bq[...] = last
        if j == 2:
            o_bv[...] = last
        loads[8 + j].wait()
        total = total + mm(sums.astype(BF16), w[...], 1, 1)
    loads[6].wait()
    total = total + jnp.concatenate([small[i // 4, i % 4] for i in range(8)], axis=0)
    o_we[...] = total[:look]
    o_be[...] = total[look:look + 1]

    def vector(i):
        i = look + i
        return small[i // 64, (i // 16) % 4, i % 16:i % 16 + 1, :]

    o_bo[...] = vector(0)
    for o, i in (
        (o_g1, S_GAIN1), (o_s1, S_SHIFT1), (o_bd, S_DOWN), (o_g2, S_GAIN2), (o_s2, S_SHIFT2)
    ):
        o[...] = vector(i)
    for i in range(4):
        o_bu[:, i * width:(i + 1) * width] = vector(S_UP + i)
    for cp in stores[8:]:
        cp.start()
    loads[5].wait()
    for i in range(8):
        o_o[i * r:(i + 1) * r, :] = out[i // 4, i % 4].astype(F32)
    stores[7].start()
    for i in range(4):
        loads[i].wait()
        stores[i].start()
    for cp in stores:
        cp.wait()


def body(
    series, embed_weight, embed_bias, query_weight, query_bias, key_weight, value_weight,
    value_bias, out_weight, out_bias, first_gain, first_shift, up_weight, up_bias,
    down_weight, down_bias, second_gain, second_shift, cotangent,
    *, dp_size, tensor_size,
):
    windows, rows, look = series.shape
    width = embed_weight.shape[1]
    hidden = up_weight.shape[0]
    pairs = HEADS // 2
    assert windows == tensor_size == 4 and width == hidden == HEADS * 64
    assert dp_size % 2 == 0 and look % 16 == 0 and look + S_UP + 4 <= 128
    padded = -(-rows // 32) * 32
    n = tensor_size * padded
    nz = dp_size // 2
    fr = width // dp_size
    r = width // 8
    half = hidden // 2

    def scr(*shape, dtype=BF16):
        return pltpu.VMEM(shape, dtype)

    scratch = [
        scr(4, 128, rows),
        scr(n, 256),
        scr(n, width, dtype=F32),
        scr(pairs, n, 512),
        scr(HEADS, n, n),
        scr(n, n),
        scr(n, width, dtype=F32),
        scr(n, width),
        scr(n, width),
        scr(n, 128, dtype=F32),
        scr(n, width),
        scr(4, n, hidden),
        scr(4, n, hidden),
        scr(4, rows, width),
        scr(n, width, dtype=F32),
        scr(n, width),
        scr(128, n),
        scr(128, n),
        scr(2, 4, hidden, width),
        scr(pairs, width, 384),
        scr(width, width),
        scr(look, width),
        scr(1 + pairs, 256, width),
        scr(4, 8, hidden, dtype=F32),
        scr(2, 4, 2, 2, nz, fr, half),
        scr(2, 2, 2, 2, nz, fr, half),
        scr(2, 2, nz, fr, half),
        scr(2, 2, nz, fr, half),
        scr(2, 2, nz, fr, half),
        scr(2, 2, nz - 1, fr, half),
        scr(pairs, 2, 4, 16, 384),
        scr(pairs, 4, 16, 384),
        scr(pairs, 3, 16, 384),
        scr(pairs, nz, 16, 384),
        scr(2, 4, r, width),
        scr(4, r, width),
        scr(3, r, width),
        scr(nz, r, width),
        scr(2, 4, 16, width, dtype=F32),
        scr(4, 16, width, dtype=F32),
        scr(3, 16, width, dtype=F32),
        scr(nz, 16, width, dtype=F32),
        scr(16, width, dtype=F32),
        scr(8, hidden, dtype=F32),
        pltpu.SemaphoreType.DMA((N_SEMS + 16 * nz,)),
        pltpu.SemaphoreType.DMA((N_SEMS + 16 * nz,)),
    ]
    hbm = pl.BlockSpec(memory_space=pl.ANY)
    vmem = pl.BlockSpec(memory_space=pltpu.VMEM)
    sd = jax.ShapeDtypeStruct
    bias = embed_bias.reshape(1, -1)
    mixed, sgrad, g_pairs, g_out, g_small, g_up, g_down = pl.pallas_call(
        functools.partial(kernel, (4, rows, padded, nz, fr)),
        out_shape=[
            sd((4, rows, width), BF16),
            sd((4, look, rows), BF16),
            sd((pairs, 2, 4, 16, 384), BF16),
            sd((2, 4, r, width), BF16),
            sd((2, 4, 16, width), F32),
            sd((fr, hidden), F32),
            sd((fr, hidden), F32),
        ],
        in_specs=[hbm] * 9 + [vmem] * 10,
        out_specs=[hbm] * 2 + [vmem] * 5,
        scratch_shapes=scratch,
        compiler_params=pltpu.CompilerParams(
            collective_id=1, has_side_effects=True, vmem_limit_bytes=64 * 1024 * 1024
        ),
    )(
        jnp.swapaxes(series, 1, 2), cotangent, embed_weight, query_weight, key_weight,
        value_weight, out_weight, up_weight, down_weight, bias,
        *(v.reshape(1, -1) for v in (
            query_bias, value_bias, out_bias, first_gain, first_shift, down_bias,
            second_gain, second_shift, up_bias,
        )),
    )
    vector = sd((1, width), F32)
    operands = (
        mixed, sgrad, g_up, g_down, g_pairs, g_out, g_small, embed_weight, query_weight,
        key_weight, value_weight, bias,
    )
    made = [
        *[sd((width, width), F32)] * 4,
        sd((look, width), F32),
        *[vector] * 6,
        sd((1, 4 * hidden), F32),
        *[vector] * 3,
    ]
    out = pl.pallas_call(
        functools.partial(finish, (pairs, len(operands), 4 + len(made))),
        out_shape=[sd(a.shape, a.dtype) for a in operands[:4]] + made,
        in_specs=[hbm] * len(operands),
        out_specs=[hbm] * (4 + len(made)),
        scratch_shapes=[
            *[scr(*a.shape, dtype=a.dtype) for a in operands],
            *[scr(*a.shape, dtype=a.dtype) for a in made],
            pltpu.SemaphoreType.DMA((len(operands),)),
            pltpu.SemaphoreType.DMA((4 + len(made),)),
        ],
        compiler_params=pltpu.CompilerParams(vmem_limit_bytes=64 * 1024 * 1024),
    )(*operands)
    mixed, sgrad, g_up, g_down, g_q, g_k, g_v, g_o, g_e = out[:9]
    g_be, g_bq, g_bv, g_bo, g_g1, g_s1, g_bu, g_bd, g_g2, g_s2 = (
        v.reshape(-1) for v in out[9:]
    )
    return (
        mixed, jnp.swapaxes(sgrad, 1, 2), g_e, g_be, g_q, g_bq, g_k, g_v, g_bv, g_o, g_bo,
        g_g1, g_s1, g_up.T, g_bu, g_down.T, g_bd, g_g2, g_s2,
    )


def solution(mesh):
    token = P("dp", "tensor", None)
    return jax.shard_map(
        functools.partial(
            body, dp_size=mesh.shape["dp"], tensor_size=mesh.shape["tensor"]
        ),
        mesh=mesh,
        in_specs=(
            token, P(), P(), P(), P(), P(), P(), P(), P(), P(), P(), P(),
            P("tensor", None), P("tensor"), P("tensor", None), P(), P(), P(), token,
        ),
        out_specs=(
            token, token, P(), P(), P(), P(), P(), P(), P(), P(), P(), P(), P(),
            P("tensor", "dp"), P(), P("tensor", "dp"), P(), P(), P(),
        ),
        check_vma=False,
    )
```

```python
import functools
import jax
import jax.numpy as jnp
from jax import lax
from jax.experimental import pallas as pl
from jax.experimental.pallas import tpu as pltpu
from jax.sharding import PartitionSpec as P

HEADS = 8
EPSILON = 1e-05
F32 = jnp.float32
BF16 = jnp.bfloat16
MESH = pl.DeviceIdType.MESH
GELU_A = 0.7978845608028654
GELU_B = GELU_A * 0.044715
MASKED = -1e30

EMBED, QUERY, VALUE, OUT, GAIN1, SHIFT1, DOWN, GAIN2, SHIFT2 = range(9)
S_GAIN1, S_SHIFT1, S_DOWN, S_GAIN2, S_SHIFT2, S_UP = range(1, 7)


def mm(left, right, cl=1, cr=0):
    return lax.dot_general(
        left, right, (((cl,), (cr,)), ((), ())), preferred_element_type=F32
    )


def row_mean(x):
    return jnp.mean(x, axis=1, keepdims=True)


def col_sum(x):
    return jnp.sum(x, axis=0, keepdims=True)


def pad_rows(x, rows):
    if x.shape[0] == rows:
        return x
    return jnp.concatenate([x, jnp.zeros((rows - x.shape[0], x.shape[1]), x.dtype)], axis=0)


class Copy:
    def __init__(self, sems, make):
        self.sems, self.make, self.copy = sems, make, None

    def reserve(self):
        self.slot = self.sems.take()
        self.copy = self.make(self.sems.send.at[self.slot])

    def start(self):
        if self.copy is None:
            self.reserve()
        self.copy.start()

    def wait_recv(self):
        self.copy.wait_recv()

    def wait_send(self):
        self.copy.wait_send()
        self.sems.free.append(self.slot)

    def wait(self):
        self.copy.wait()
        self.sems.free.append(self.slot)


class Sems:
    def __init__(self, send, recv):
        self.send, self.recv = send, recv
        self.free = list(range(send.shape[0]))[::-1]
        self.used = 0

    def take(self):
        return self.free.pop()

    def copy(self, src, dst, device):
        i = self.used
        self.used += 1
        assert i < self.recv.shape[0]
        return Copy(self, lambda sem: pltpu.make_async_remote_copy(
            src_ref=src,
            dst_ref=dst,
            send_sem=sem,
            recv_sem=self.recv.at[i],
            device_id=device,
            device_id_type=MESH,
        ))

    def local(self, src, dst):
        return Copy(self, lambda sem: pltpu.make_async_copy(src, dst, sem))


N_SEND, N_SEND_Z = 44, 8
N_RECV, N_RECV_Z = 96, 10

AXES = {"d0": "xy", "d1": "yxz", "u0": "zxy", "u1": "zyx"}
DIRECT = ("p3",)
SCHEDULE = {
    "dk3": ("m",),
    "uk0": ("d0", "d0", "d1",),
    "uk1": ("d1",),
    "uk2": ("u0", "u1",),
    "uk3": ("u0", "u1",),
    "n1": ("d0",),
    "a0b": ("S", "O", "d1",),
    "a1a": ("u0", "d0", "p0", "m",),
    "a1w": ("S",),
    "a2a": ("p1", "u1",),
    "a2b": ("O",),
    "a3a": ("d0", "d1", "p2",),
    "a3w": ("S",),
    "sb": ("u0", "p1", "p0",),
    "end": (
        "u1", "p2", "O", "p3", "d1", "u1", "S", "p1", "u0", "S",
        "p0", "p2", "p3", "O", "p1", "d1", "p0", "O", "p2", "p1",
        "p0", "u1", "p2", "p3", "u0",
    ),
}


def kernel(
    cfg,
    series, cot_in, w_embed, w_q, w_k, w_v, w_o, w_up, w_down,
    b_embed, b_query, b_value, b_out, gain1, shift1, b_down, gain2, shift2, b_up,
    o_mixed, o_series, h_pairs, h_out, h_small, h_up, h_down,
    xs, xa, en, qkv, prob, ds, mxf, mx, rinv, inv1, flow, hid, slope, cot, g2, gb,
    qt, dt, wb, wqkv, wo, we, w2, ubb,
    g, rc, r1, r2, r3, rz,
    gp_, gprc, gpr1, gprz,
    go, gorc, gor1, gorz,
    gs, gsrc, gsr1, gsrz,
    o_pairs, o_out, o_small, o_up, o_down, vec, upv, ubl, send, recv,
):
    blocks, rows, padded, nz, fr = cfg
    n = blocks * padded
    look = we.shape[0]
    width = wo.shape[0]
    pairs = qkv.shape[0]
    hidden = w_up.shape[0]
    lanes2 = hidden // 2
    dp, t = lax.axis_index("dp"), lax.axis_index("tensor")
    c, y = t % 2, t // 2
    b, z = dp % 2, dp // 2
    co, yo, bo = 1 - c, 1 - y, 1 - b
    xy = y * 2 + b
    sems = Sems(send, recv)

    def dev(cc, yy, bb, zz=None):
        return ((z if zz is None else zz) * 2 + bb, yy * 2 + cc)

    core_dev, y_dev, x_dev = dev(co, y, b), dev(c, yo, b), dev(c, y, bo)
    xy_peers = [(y, bo), (yo, b), (yo, bo)]

    barrier = pltpu.get_barrier_semaphore()
    partners = [core_dev]
    partners += [dev(cc, py, pb) for cc in (c, co) for py, pb in xy_peers]
    partners += [dev(c, y, b, (z + k) % nz) for k in range(1, nz)]
    for partner in partners:
        pl.semaphore_signal(barrier, inc=1, device_id=partner, device_id_type=MESH)

    def load(src, dst):
        cp = sems.local(src, dst)
        cp.start()
        return cp

    load_vec = [load(b_up, upv)]
    for i, ref in enumerate(
        (b_embed, b_query, b_value, b_out, gain1, shift1, b_down, gain2, shift2)
    ):
        load_vec.append(load(ref, vec.at[i]))
    load_we = load(w_embed, we)
    load_qkv = []
    for p in range(pairs):
        for j, w in enumerate((w_q, w_k, w_v)):
            load_qkv.append(load(
                w.at[:, 128 * p:128 * p + 128], wqkv.at[p, :, 128 * j:128 * j + 128]
            ))
    own_x = load(series.at[t], xs.at[t, 0:look])
    own_w = [load(w, wb.at[m, t]) for m, w in enumerate((w_up, w_down))]
    load_wo = load(w_o, wo)
    own_cot = load(cot_in.at[t], cot.at[t])
    for cp in load_vec:
        cp.wait()
    ubl[...] = jnp.broadcast_to(upv[...].astype(F32), ubl.shape)
    ubb[t] = ubl[...]
    tail_rows = xs.shape[1] - look
    first = lax.broadcasted_iota(jnp.int32, (tail_rows, rows), 0) == 0
    for i in range(blocks):
        xs[i, look:, :] = jnp.where(first, 1.0, 0.0).astype(BF16)

    pl.semaphore_wait(barrier, len(partners))

    def exchange(src, dst, dst_at):
        out = []
        for k in range(1, blocks):
            other = (t + k) % blocks
            out.append(sems.copy(src.at[other], dst_at(dst), (dp, other)))
        return out

    send_x = exchange(series, xs, lambda r: r.at[t, 0:look])
    part = hidden // 4
    t_y, t_c, t_d = yo * 2 + c, y * 2 + co, yo * 2 + co
    stage_y, stage_core, stage_ub, stage_x, stage_d, stage_e = [], [], [], [], [], []
    for s in range(2):
        at = pl.ds(pl.multiple_of((b * 2 + s) * part, part), part)
        far = pl.ds(pl.multiple_of((bo * 2 + s) * part, part), part)
        for m, w in enumerate((w_up, w_down)):
            stage_y.append(sems.copy(w.at[at], wb.at[m, t, at], y_dev))
            stage_x.append(sems.copy(wb.at[m, t_y, at], wb.at[m, t_y, at], x_dev))
            stage_d.append(sems.copy(wb.at[m, t_y, at], wb.at[m, t_y, at], core_dev))
            stage_e.append(sems.copy(wb.at[m, t_y, far], wb.at[m, t_y, far], core_dev))
    for m, w in enumerate((w_up, w_down)):
        stage_core.append(sems.copy(w, wb.at[m, t], core_dev))
    for k in range(1, blocks):
        other = (t + k) % blocks
        stage_ub.append(sems.copy(ubl, ubb.at[t], (dp, other)))
    send_cot = exchange(cot_in, cot, lambda r: r.at[t])
    for cp in send_x + stage_ub + stage_y + stage_core + send_cot:
        cp.start()

    for cp in stage_x + stage_d + stage_e:
        cp.reserve()

    def forward_y(i):
        stage_y[i].wait_recv()
        stage_x[i].start()
        stage_d[i].start()

    def forward_x(i):
        stage_x[i].wait_recv()
        stage_e[i].start()

    load_we.wait()
    one_row = lax.broadcasted_iota(jnp.int32, (128, 1), 0)
    b_high = vec[EMBED].astype(BF16)
    b_low = vec[EMBED] - b_high.astype(F32)
    we_rows = pad_rows(we[...].astype(F32), 128)
    high = we_rows + jnp.where(one_row == look, b_high.astype(F32), 0.0)
    low = jnp.where(one_row == look, b_low, 0.0)
    w2[0, 0:128, :] = high.astype(BF16)
    w2[0, 128:256, :] = low.astype(BF16)
    both = (high + jnp.where(one_row == look + 1, b_low, 0.0)).astype(BF16)
    for cp in load_qkv:
        cp.wait()
    for p in range(pairs):
        at = slice(128 * p, 128 * p + 128)
        prod = mm(both, wqkv[p])
        bias = prod[look:look + 1] + prod[look + 1:look + 2]
        bias = bias + jnp.concatenate(
            [vec[QUERY, :, at], jnp.zeros((1, 128), F32), vec[VALUE, :, at]],
            axis=1,
        )
        prod = jnp.where(one_row < look, prod, jnp.where(one_row == look, bias, 0.0))
        factor = lax.broadcasted_iota(jnp.int32, (1, 384), 1)
        prod = prod * jnp.where(factor < 128, 0.125, 1.0)
        high = prod.astype(BF16)
        w2[1 + p, 0:128, 0:384] = high
        w2[1 + p, 128:256, 0:384] = (prod - high.astype(F32)).astype(BF16)
        qkv[p, :, 384:512] = jnp.ones((n, 128), BF16)

    own_x.wait()
    for cp in send_x:
        cp.wait()
    for i in range(blocks):
        x = pad_rows(xs[i].astype(F32).T, padded).astype(BF16)
        at = pl.ds(i * padded, padded)
        xa[at, 0:128] = x
        xa[at, 128:256] = x
    en[...] = mm(xa[...], w2[0])

    def project(p, carry):
        qkv[p, :, 0:384] = mm(xa[...], w2[1 + p, :, 0:384]).astype(BF16)
        return carry

    lax.fori_loop(0, pairs, project, 0)

    lane = lax.broadcasted_iota(jnp.int32, (1, 128), 1)
    key_at = lax.broadcasted_iota(jnp.int32, (1, n), 1)
    mask = jnp.where(key_at % padded >= rows, MASKED, 0.0).astype(F32)

    tile_f = 128

    def attend_pair(p, carry):
        for k, do in enumerate(((forward_y, 0), (forward_y, 1), (forward_y, 2), (forward_y, 3))):
            pl.when(p == k)(functools.partial(*do))
        pl.when(p == 3)(functools.partial(forward_x, 0))

        def attend_tile(i, carry):
            at = pl.ds(pl.multiple_of(i * tile_f, tile_f), tile_f)
            q = qkv[p, at, 0:128]
            outs, inverses = [], []
            for h in range(2):
                qm = jnp.where((lane // 64) == h, q, jnp.zeros_like(q))
                s = mm(qm, qkv[p, :, 128:256], 1, 1) + mask
                e = jnp.exp(s - jnp.max(s, axis=1, keepdims=True)).astype(BF16)
                prob[2 * p + h, at, :] = e
                o = mm(e, qkv[p, :, 256:512])
                outs.append(o[:, :128])
                inverses.append(1.0 / o[:, 128:])
            inverse = jnp.where(lane < 64, inverses[0], inverses[1])
            o = jnp.where(lane < 64, outs[0], outs[1]) * inverse
            lanes = pl.ds(pl.multiple_of(p * 128, 128), 128)
            mxf[at, lanes] = o
            mx[at, lanes] = o.astype(BF16)
            rinv[at, lanes] = inverse.astype(BF16)
            return carry

        lax.fori_loop(0, n // tile_f, attend_tile, 0, unroll=True)
        return carry

    lax.fori_loop(0, pairs, attend_pair, 0)
    forward_x(1)
    forward_x(2)

    load_wo.wait()

    def first_norm(i, carry):
        at = pl.ds(pl.multiple_of(i * padded, padded), padded)
        zz = en[at, :] + (mm(mx[at, :], wo[...]) + vec[OUT])
        centred = zz - row_mean(zz)
        inv = lax.rsqrt(row_mean(centred * centred) + EPSILON)
        nn = centred * inv
        en[at, :] = nn
        inv1[at, :] = jnp.broadcast_to(inv, (padded, 128))
        out = nn * vec[GAIN1] + vec[SHIFT1]
        flow[at, :] = out.astype(BF16)
        g2[at, :] = out + vec[DOWN]
        return carry

    lax.fori_loop(0, blocks, first_norm, 0)
    forward_x(3)

    tile_h = n // 2

    def feed_forward(j):
        for i in range(n // tile_h):
            at = slice(i * tile_h, (i + 1) * tile_h)
            v = mm(flow[at, :], wb[0, j], 1, 1) + ubb[j, 0:1, :]
            v2 = v * v
            half = 0.5 * jnp.tanh(v * (GELU_A + GELU_B * v2)) + 0.5
            h = v * half
            slope[j, at, :] = (
                half + h * (1.0 - half) * (2 * GELU_A + (6 * GELU_B) * v2)
            ).astype(BF16)
            h = h.astype(BF16)
            hid[j, at, :] = h
            g2[at, :] += mm(h, wb[1, j])

    for cp in own_w:
        cp.wait()
    feed_forward(t)
    for cp in stage_core + stage_ub:
        cp.wait()
    feed_forward(t_c)
    for cp in stage_x + stage_y:
        cp.wait_send()
    feed_forward(t_y)
    for cp in stage_d + stage_e:
        cp.wait()
    feed_forward(t_d)

    own_cot.wait()
    for cp in send_cot:
        cp.wait()

    def add_row(row, value, at=slice(None)):
        i = look + row
        gs[i // 64, (i // 16) % 4, i % 16:i % 16 + 1, at] += value

    gs[...] = jnp.zeros_like(gs)

    def second_norm(i, carry):
        at = pl.ds(pl.multiple_of(i * padded, padded), padded)
        acc = g2[at, :]
        centred = acc - row_mean(acc)
        inv = lax.rsqrt(row_mean(centred * centred) + EPSILON)
        nn = centred * inv
        up = pad_rows(cot[i].astype(F32), padded)
        result = nn * vec[GAIN2] + vec[SHIFT2]
        cot[i] = result[:rows].astype(BF16)
        gg = up * vec[GAIN2]
        back = inv * (gg - row_mean(gg) - nn * row_mean(gg * nn))
        g2[at, :] = back
        low = back.astype(BF16)
        gb[at, :] = low
        add_row(S_GAIN2, col_sum(up * nn))
        add_row(S_SHIFT2, col_sum(up))
        add_row(S_DOWN, col_sum(low.astype(F32)))
        return carry

    lax.fori_loop(0, blocks, second_norm, 0)
    own_mixed = sems.local(cot.at[t], o_mixed.at[t])
    own_mixed.start()
    send_mixed = [
        sems.copy(cot.at[other], o_mixed.at[t], (dp, other)) for other in (t_c, t_y, t_d)
    ]
    send_mixed[0].start()
    send_mixed_y = send_mixed[1:]

    def add_into(dst, src, index):
        dst[index] = (dst[index].astype(F32) + src[...].astype(F32)).astype(dst.dtype)

    results = []

    class Sum:
        def start(self, src, dst, device):
            cp = sems.copy(src, dst, device)
            cp.start()
            self.cps.append(cp)

        def wait(self):
            for cp in self.cps:
                cp.wait()
            self.cps = []

    def free_axes(order):
        axes = [a for a in order if a != "y"]
        return axes if "z" in axes else axes + ["z"]

    mine, theirs = {"x": b, "z": z % 2}, {"x": bo, "z": 1 - z % 2}
    z_near = z + 1 - 2 * (z % 2)
    axis_dev = {"y": y_dev, "x": x_dev, "z": dev(c, y, b, z_near)}

    class FeedSum(Sum):
        def __init__(self, m, h, axes, out):
            self.m, self.h, self.axes, self.out = m, h, axes, out
            self.free = free_axes(axes)
            self.core = []
            self.cps = []

        def at(self, *index):
            return (self.m, self.h) + index

        def send_core(self, k):
            cp = sems.copy(g.at[self.at(k)], rc.at[self.at(k)], core_dev)
            cp.start()
            self.core.append(cp)

        def add_core(self, k):
            self.core[k - 2].wait()
            add_into(g, rc.at[self.at(k - 2)], self.at(k))

        def send(self, axis, slices, fixed, to):
            for i, k in enumerate(slices):
                src = g.at[self.at(k, *fixed)]
                dst = to
                if axis != "y":
                    src = g.at[self.at(k, *fixed, theirs[axis])]
                    dst = to if len(slices) == 1 else to.at[i]
                self.start(src, dst, axis_dev[axis])

        def steps(self):
            m, h = self.m, self.h
            stages = [r1.at[m, h], r2.at[m, h], r3.at[m, h]]
            axes, fixed, slices = self.axes, [], [2, 3]
            self.add_core(2)
            if axes[0] == "y":
                self.send("y", [2], [], stages[0])
            else:
                self.start(
                    g.at[self.at(2, theirs[axes[0]])], stages[0].at[0], axis_dev[axes[0]]
                )
            yield
            self.add_core(3)
            if axes[0] != "y":
                self.start(
                    g.at[self.at(3, theirs[axes[0]])], stages[0].at[1], axis_dev[axes[0]]
                )
            yield
            for i, axis in enumerate(axes):
                self.wait()
                if axis == "y":
                    slices = [3]
                    add_into(g, stages[i], self.at(3, *fixed))
                else:
                    fixed = fixed + [mine[axis]]
                    for j, k in enumerate(slices):
                        got = stages[i] if len(slices) == 1 else stages[i].at[j]
                        add_into(g, got, self.at(k, *fixed))
                if i + 1 < len(axes):
                    nxt = axes[i + 1]
                    self.send(nxt, [2] if nxt == "y" else slices, fixed, stages[i + 1])
                    yield
            if "z" in axes:
                far = [((z // 2 + k) % (nz // 2)) for k in range(1, nz // 2)]
                parts = [(dev(c, y, b, f * 2 + z % 2), fixed + [f]) for f in far]
                own = fixed + [z // 2]
            else:
                far = [(z + k) % nz for k in range(1, nz)]
                parts = [(dev(c, y, b, f), fixed + [f % 2, f // 2]) for f in far]
                own = fixed + [z % 2, z // 2]
            for k, (to, at) in enumerate(parts):
                self.start(g.at[self.at(3, *at)], rz.at[m, h, k], to)
            yield
            self.wait()
            total = g[self.at(3, *own)].astype(F32)
            for k in range(len(parts)):
                total = total + rz[m, h, k].astype(F32)
            at = (slice(None), slice(h * lanes2, (h + 1) * lanes2))
            self.out[0][at] = total
            results.append(load(self.out[0].at[at], self.out[1].at[at]))

    class WholeSum(Sum):
        def __init__(self, key, grad, rcv, rcv1, rcvz, out, result):
            self.direct = key in DIRECT
            self.refs = (grad, rcv, rcv1, rcvz, out)
            self.result = result

        def steps(self):
            grad, rcv, rcv1, rcvz, out = self.refs
            self.cps = []
            if self.direct:
                for k, (py, pb) in enumerate([(y, b)] + xy_peers):
                    self.start(grad.at[co, py * 2 + pb], rcv.at[k], dev(co, py, pb))
            else:
                self.start(grad.at[co], rcv, core_dev)
                yield
                self.wait()
                for i in range(4):
                    add_into(grad, rcv.at[i], (c, i))
            for k, (py, pb) in enumerate(xy_peers):
                self.start(grad.at[c, py * 2 + pb], rcv1.at[k], dev(c, py, pb))
            yield
            self.wait()
            total = grad[c, xy].astype(F32)
            for k in range(3):
                total = total + rcv1[k].astype(F32)
            if self.direct:
                for k in range(4):
                    total = total + rcv[k].astype(F32)
            rcvz[z] = total.astype(grad.dtype)
            for k in range(1, nz):
                self.start(rcvz.at[z], rcvz.at[z], dev(c, y, b, (z + k) % nz))
            yield
            self.wait()
            total = rcvz[0].astype(F32)
            for k in range(1, nz):
                total = total + rcvz[k].astype(F32)
            out[c, xy] = total.astype(grad.dtype)
            for py, pb in xy_peers:
                self.start(out.at[c, xy], out.at[c, xy], dev(c, py, pb))
            if self.direct:
                for py, pb in [(y, b)] + xy_peers:
                    self.start(out.at[c, xy], out.at[c, xy], dev(co, py, pb))
            else:
                yield
                self.wait()
                self.start(out.at[c], out.at[c], core_dev)
            yield
            self.wait()
            results.append(load(out, self.result))

    chains = {}
    feeds = {}
    for m, (name, out) in enumerate((("d", (o_down, h_down)), ("u", (o_up, h_up)))):
        for h in range(2):
            key = name + str(h)
            feeds[key] = FeedSum(m, h, AXES[key], out)

    def point(name):
        for key in SCHEDULE.get(name, ()):
            if key == "m":
                send_mixed_y.pop(0).start()
            else:
                if key not in chains:
                    chains[key] = feeds[key].steps()
                next(chains[key], None)

    order = (t_d, t_c, t_y, t)

    def feed_grad(m, k, left, right):
        out = mm(left, right, 0, 0).astype(BF16)
        for h in range(2):
            for zz in range(nz):
                for bb in range(2):
                    i = (zz * 2 + bb) * fr
                    at = {"x": bb, "z": zz % 2}
                    at = tuple(at[a] for a in feeds["du"[m] + str(h)].free)
                    g[(m, h, k) + at + (zz // 2,)] = out[i:i + fr, h * lanes2:(h + 1) * lanes2]

    point("n2")

    for k, j in enumerate(order):
        feed_grad(0, k, gb[...], hid[j])
        if k < 2:
            feeds["d0"].send_core(k)
            feeds["d1"].send_core(k)
        point("dk" + str(k))

    def feed_back(k, j):
        for i in range(n // tile_h):
            at = slice(i * tile_h, (i + 1) * tile_h)
            gp = (slope[j, at, :].astype(F32) * mm(gb[at, :], wb[1, j], 1, 1)).astype(BF16)
            slope[j, at, :] = gp
            g2[at, :] += mm(gp, wb[0, j])
        up_rows[k] = col_sum(slope[j].astype(F32))
        feed_grad(1, k, flow[...], slope[j])

    up_rows = [None] * blocks
    for k, j in enumerate(order):
        feed_back(k, j)
        if k < 2:
            feeds["u0"].send_core(k)
            feeds["u1"].send_core(k)
        point("uk" + str(k))
    for k, j in enumerate(order):
        i = look + S_UP + j
        gs[i // 64, (i // 16) % 4, pl.ds(i % 16, 1), :] = up_rows[k]

    def first_back(i, carry):
        at = pl.ds(pl.multiple_of(i * padded, padded), padded)
        acc = g2[at, :]
        nn = en[at, :]
        add_row(S_GAIN1, col_sum(acc * nn))
        add_row(S_SHIFT1, col_sum(acc))
        gg = acc * vec[GAIN1]
        inv = inv1[at, 0:1]
        back = inv * (gg - row_mean(gg) - nn * row_mean(gg * nn))
        ga = back.astype(BF16)
        hid[0, at, :] = ga
        gm = mm(ga, wo[...], 1, 1)
        gb[at, :] = (gm * rinv[at, :].astype(F32)).astype(BF16)
        return carry

    lax.fori_loop(0, blocks, first_back, 0)
    point("n1")

    ga = hid.at[0]
    out_grad = mm(mx[...], ga[...], 0, 0).astype(BF16)
    for i in range(8):
        r = width // 8
        go[i // 4, i % 4] = out_grad[i * r:(i + 1) * r]
    chains["O"] = WholeSum("O", go, gorc, gor1, gorz, o_out, h_out).steps()
    next(chains["O"])
    small = mm(xa[:, 0:128], ga[...], 0, 0)
    for i in range(8):
        gs[i // 4, i % 4] += small[16 * i:16 * i + 16]
    chains["S"] = WholeSum("S", gs, gsrc, gsr1, gsrz, o_small, h_small).steps()
    next(chains["S"])
    point("og")

    tile_b = n // 2

    def attend_back(p):
        lanes = pl.ds(p * 128, 128)
        qt[...] = qkv[p, :, 0:128].T
        dt[...] = gb[:, lanes].T
        for h in range(2):
            def tile(i, carry):
                at = pl.ds(pl.multiple_of(i * tile_b, tile_b), tile_b)
                d = gb[at, lanes]
                own = (lane // 64) == h
                dm = jnp.where(own, d, jnp.zeros_like(d))
                centre = jnp.sum(
                    jnp.where(own, d.astype(F32) * mxf[at, lanes], 0.0), axis=1, keepdims=True
                )
                s = (mm(dm, qkv[p, :, 256:384], 1, 1) - centre).astype(BF16)
                s = s * prob[2 * p + h, at, :]
                ds[at, :] = s
                dq = mm(s, qkv[p, :, 128:256])
                if h == 0:
                    mxf[at, lanes] = jnp.where(lane < 64, dq, mxf[at, lanes])
                else:
                    rinv[at, lanes] = jnp.where(lane < 64, mxf[at, lanes], dq).astype(BF16)
                return carry

            lax.fori_loop(0, n // tile_b, tile, 0, unroll=True)
            half = slice(64 * h, 64 * h + 64)
            dk = mm(qt[half, :], ds[...])
            dv = mm(dt[half, :], prob[2 * p + h])
            qt[half, :] = dk.astype(BF16)
            dt[half, :] = dv.astype(BF16)
            point("a" + str(p) + "ab"[h])
        qkv[p, :, 0:128] = rinv[:, lanes]
        qkv[p, :, 128:256] = qt[...].T
        qkv[p, :, 256:384] = dt[...].T
        grad = mm(xa[:, 0:128], qkv[p, :, 0:384], 0, 0).astype(BF16)
        for i in range(8):
            gp_[p, i // 4, i % 4] = grad[16 * i:16 * i + 16]
        key = "p" + str(p)
        chains[key] = WholeSum(
            key, gp_.at[p], gprc.at[p], gpr1.at[p], gprz.at[p], o_pairs.at[p], h_pairs.at[p]
        ).steps()
        next(chains[key])
        point("a" + str(p) + "w")

    attend_back(0)
    attend_back(1)
    attend_back(2)
    attend_back(3)

    out = mm(we[...], ga[...], 1, 1)
    for p in range(pairs):
        out = out + mm(w2[1 + p, 0:look, 0:384], qkv[p, :, 0:384], 1, 1)
    for i in range(blocks):
        xs[i, 0:look, :] = out[:, i * padded:i * padded + rows].astype(BF16)
    own_s = sems.local(xs.at[t, 0:look], o_series.at[t])
    own_s.start()
    send_s = []
    for k in range(1, blocks):
        other = (t + k) % blocks
        send_s.append(sems.copy(xs.at[other, 0:look], o_series.at[t], (dp, other)))
    for cp in send_s:
        cp.start()
    point("sb")
    point("end")
    while send_mixed_y:
        send_mixed_y.pop(0).start()
    for _ in range(6):
        for key in chains:
            next(chains[key], None)
    for cp in send_s + send_mixed:
        cp.wait()
    for cp in results + [own_s, own_mixed]:
        cp.wait()


def finish(cfg, *refs):
    pairs, n_in, n_out = cfg
    inputs, refs = refs[:n_in], refs[n_in:]
    results, refs = refs[:n_out], refs[n_out:]
    held, refs = refs[:n_in], refs[n_in:]
    made, (sem_in, sem_out) = refs[:-2], refs[-2:]
    mixed, sgrad, up, down, pair_sums, out, small, we, wq, wk, wv, be = held
    made = (mixed, sgrad, up, down) + tuple(made)
    loads = [
        pltpu.make_async_copy(src, dst, sem_in.at[i])
        for i, (src, dst) in enumerate(zip(inputs, held))
    ]
    stores = [
        pltpu.make_async_copy(src, dst, sem_out.at[i])
        for i, (src, dst) in enumerate(zip(made, results))
    ]
    o_q, o_k, o_v, o_o, o_we, o_be, o_bq, o_bv, o_bo, o_g1, o_s1, o_bu, o_bd, o_g2, o_s2 = made[4:]
    for i in (4, 7, 11, 8, 9, 10, 6, 5, 0, 1, 2, 3):
        loads[i].start()
    look, width = we.shape
    r = width // 8
    for i in (4, 7, 11):
        loads[i].wait()
    row = lax.broadcasted_iota(jnp.int32, (128, 1), 0)
    b_high = be[...].astype(BF16).astype(F32)
    left = pad_rows(we[...].astype(F32), 128)
    left = left + jnp.where(row == look, b_high, 0.0)
    left = (left + jnp.where(row == look + 1, be[...] - b_high, 0.0)).astype(BF16)
    total = jnp.zeros((128, width), F32)
    for j, (o, w) in enumerate(((o_q, wq), (o_k, wk), (o_v, wv))):
        sums = jnp.concatenate(
            [
                jnp.concatenate(
                    [pair_sums[p, i // 4, i % 4, :, 128 * j:128 * j + 128] for i in range(8)],
                    axis=0,
                ).astype(F32)
                for p in range(pairs)
            ],
            axis=1,
        )
        if j == 0:
            sums = sums * 0.125
        last = sums[look:look + 1]
        o[...] = mm(left, (sums + jnp.where(row == look + 1, last, 0.0)).astype(BF16), 0, 0)
        stores[4 + j].start()
        if j == 0:
            o_bq[...] = last
        if j == 2:
            o_bv[...] = last
        loads[8 + j].wait()
        total = total + mm(sums.astype(BF16), w[...], 1, 1)
    loads[6].wait()
    total = total + jnp.concatenate([small[i // 4, i % 4] for i in range(8)], axis=0)
    o_we[...] = total[:look]
    o_be[...] = total[look:look + 1]

    def vector(i):
        i = look + i
        return small[i // 64, (i // 16) % 4, i % 16:i % 16 + 1, :]

    o_bo[...] = vector(0)
    for o, i in (
        (o_g1, S_GAIN1), (o_s1, S_SHIFT1), (o_bd, S_DOWN), (o_g2, S_GAIN2), (o_s2, S_SHIFT2)
    ):
        o[...] = vector(i)
    for i in range(4):
        o_bu[:, i * width:(i + 1) * width] = vector(S_UP + i)
    for cp in stores[8:]:
        cp.start()
    loads[5].wait()
    for i in range(8):
        o_o[i * r:(i + 1) * r, :] = out[i // 4, i % 4].astype(F32)
    stores[7].start()
    for i in range(4):
        loads[i].wait()
        stores[i].start()
    for cp in stores:
        cp.wait()


def body(
    series, embed_weight, embed_bias, query_weight, query_bias, key_weight, value_weight,
    value_bias, out_weight, out_bias, first_gain, first_shift, up_weight, up_bias,
    down_weight, down_bias, second_gain, second_shift, cotangent,
    *, dp_size, tensor_size,
):
    windows, rows, look = series.shape
    width = embed_weight.shape[1]
    hidden = up_weight.shape[0]
    pairs = HEADS // 2
    assert windows == tensor_size == 4 and width == hidden == HEADS * 64
    assert dp_size % 4 == 0 and look % 16 == 0 and look + S_UP + 4 <= 128
    padded = -(-rows // 32) * 32
    n = tensor_size * padded
    nz = dp_size // 2
    fr = width // dp_size
    r = width // 8
    half = hidden // 2

    def scr(*shape, dtype=BF16):
        return pltpu.VMEM(shape, dtype)

    scratch = [
        scr(4, 128, rows),
        scr(n, 256),
        scr(n, width, dtype=F32),
        scr(pairs, n, 512),
        scr(HEADS, n, n),
        scr(n, n),
        scr(n, width, dtype=F32),
        scr(n, width),
        scr(n, width),
        scr(n, 128, dtype=F32),
        scr(n, width),
        scr(4, n, hidden),
        scr(4, n, hidden),
        scr(4, rows, width),
        scr(n, width, dtype=F32),
        scr(n, width),
        scr(128, n),
        scr(128, n),
        scr(2, 4, hidden, width),
        scr(pairs, width, 384),
        scr(width, width),
        scr(look, width),
        scr(1 + pairs, 256, width),
        scr(4, 8, hidden, dtype=F32),
        scr(2, 2, 4, 2, 2, nz // 2, fr, half),
        scr(2, 2, 2, 2, 2, nz // 2, fr, half),
        scr(2, 2, 2, 2, nz // 2, fr, half),
        scr(2, 2, 2, nz // 2, fr, half),
        scr(2, 2, nz // 2, fr, half),
        scr(2, 2, nz - 1, fr, half),
        scr(pairs, 2, 4, 16, 384),
        scr(pairs, 4, 16, 384),
        scr(pairs, 3, 16, 384),
        scr(pairs, nz, 16, 384),
        scr(2, 4, r, width),
        scr(4, r, width),
        scr(3, r, width),
        scr(nz, r, width),
        scr(2, 4, 16, width, dtype=F32),
        scr(4, 16, width, dtype=F32),
        scr(3, 16, width, dtype=F32),
        scr(nz, 16, width, dtype=F32),
        scr(pairs, 2, 4, 16, 384),
        scr(2, 4, r, width),
        scr(2, 4, 16, width, dtype=F32),
        scr(fr, hidden, dtype=F32),
        scr(fr, hidden, dtype=F32),
        scr(9, 1, width, dtype=F32),
        scr(1, hidden),
        scr(8, hidden, dtype=F32),
        pltpu.SemaphoreType.DMA((N_SEND + N_SEND_Z * nz,)),
        pltpu.SemaphoreType.DMA((N_RECV + N_RECV_Z * nz,)),
    ]
    hbm = pl.BlockSpec(memory_space=pl.ANY)
    vmem = pl.BlockSpec(memory_space=pltpu.VMEM)
    sd = jax.ShapeDtypeStruct
    bias = embed_bias.reshape(1, -1)
    mixed, sgrad, g_pairs, g_out, g_small, g_up, g_down = pl.pallas_call(
        functools.partial(kernel, (4, rows, padded, nz, fr)),
        out_shape=[
            sd((4, rows, width), BF16),
            sd((4, look, rows), BF16),
            sd((pairs, 2, 4, 16, 384), BF16),
            sd((2, 4, r, width), BF16),
            sd((2, 4, 16, width), F32),
            sd((fr, hidden), F32),
            sd((fr, hidden), F32),
        ],
        in_specs=[hbm] * 19,
        out_specs=[hbm] * 7,
        scratch_shapes=scratch,
        compiler_params=pltpu.CompilerParams(
            collective_id=1, has_side_effects=True, vmem_limit_bytes=64 * 1024 * 1024
        ),
    )(
        jnp.swapaxes(series, 1, 2), cotangent, embed_weight, query_weight, key_weight,
        value_weight, out_weight, up_weight, down_weight, bias,
        *(v.reshape(1, -1) for v in (
            query_bias, value_bias, out_bias, first_gain, first_shift, down_bias,
            second_gain, second_shift, up_bias,
        )),
    )
    vector = sd((1, width), F32)
    operands = (
        mixed, sgrad, g_up, g_down, g_pairs, g_out, g_small, embed_weight, query_weight,
        key_weight, value_weight, bias,
    )
    made = [
        *[sd((width, width), F32)] * 4,
        sd((look, width), F32),
        *[vector] * 6,
        sd((1, 4 * hidden), F32),
        *[vector] * 3,
    ]
    out = pl.pallas_call(
        functools.partial(finish, (pairs, len(operands), 4 + len(made))),
        out_shape=[sd(a.shape, a.dtype) for a in operands[:4]] + made,
        in_specs=[hbm] * len(operands),
        out_specs=[hbm] * (4 + len(made)),
        scratch_shapes=[
            *[scr(*a.shape, dtype=a.dtype) for a in operands],
            *[scr(*a.shape, dtype=a.dtype) for a in made],
            pltpu.SemaphoreType.DMA((len(operands),)),
            pltpu.SemaphoreType.DMA((4 + len(made),)),
        ],
        compiler_params=pltpu.CompilerParams(vmem_limit_bytes=64 * 1024 * 1024),
    )(*operands)
    mixed, sgrad, g_up, g_down, g_q, g_k, g_v, g_o, g_e = out[:9]
    g_be, g_bq, g_bv, g_bo, g_g1, g_s1, g_bu, g_bd, g_g2, g_s2 = (
        v.reshape(-1) for v in out[9:]
    )
    return (
        mixed, jnp.swapaxes(sgrad, 1, 2), g_e, g_be, g_q, g_bq, g_k, g_v, g_bv, g_o, g_bo,
        g_g1, g_s1, g_up.T, g_bu, g_down.T, g_bd, g_g2, g_s2,
    )


def solution(mesh):
    token = P("dp", "tensor", None)
    return jax.shard_map(
        functools.partial(
            body, dp_size=mesh.shape["dp"], tensor_size=mesh.shape["tensor"]
        ),
        mesh=mesh,
        in_specs=(
            token, P(), P(), P(), P(), P(), P(), P(), P(), P(), P(), P(),
            P("tensor", None), P("tensor"), P("tensor", None), P(), P(), P(), token,
        ),
        out_specs=(
            token, token, P(), P(), P(), P(), P(), P(), P(), P(), P(), P(), P(),
            P("tensor", "dp"), P(), P("tensor", "dp"), P(), P(), P(),
        ),
        check_vma=False,
    )
```

```python
import functools
import jax
import jax.numpy as jnp
from jax import lax
from jax.experimental import pallas as pl
from jax.experimental.pallas import tpu as pltpu
from jax.sharding import PartitionSpec as P

HEADS = 8
EPSILON = 1e-05
F32 = jnp.float32
BF16 = jnp.bfloat16
MESH = pl.DeviceIdType.MESH
GELU_A = 0.7978845608028654
GELU_B = GELU_A * 0.044715
MASKED = -1e30

EMBED, QUERY, VALUE, OUT, GAIN1, SHIFT1, DOWN, GAIN2, SHIFT2 = range(9)
S_GAIN1, S_SHIFT1, S_DOWN, S_GAIN2, S_SHIFT2, S_UP = range(1, 7)


def mm(left, right, cl=1, cr=0):
    return lax.dot_general(
        left, right, (((cl,), (cr,)), ((), ())), preferred_element_type=F32
    )


def row_mean(x):
    return jnp.mean(x, axis=1, keepdims=True)


def col_sum(x):
    return jnp.sum(x, axis=0, keepdims=True)


def pad_rows(x, rows):
    if x.shape[0] == rows:
        return x
    return jnp.concatenate([x, jnp.zeros((rows - x.shape[0], x.shape[1]), x.dtype)], axis=0)


class Copy:
    def __init__(self, sems, make):
        self.sems, self.make, self.copy = sems, make, None

    def reserve(self):
        self.slot = self.sems.take()
        self.copy = self.make(self.sems.send.at[self.slot])

    def start(self):
        if self.copy is None:
            self.reserve()
        self.copy.start()

    def wait_recv(self):
        self.copy.wait_recv()

    def wait_send(self):
        self.copy.wait_send()
        self.sems.free.append(self.slot)

    def wait(self):
        self.copy.wait()
        self.sems.free.append(self.slot)


class Sems:
    def __init__(self, send, recv):
        self.send, self.recv = send, recv
        self.free = list(range(send.shape[0]))[::-1]
        self.used = 0

    def take(self):
        return self.free.pop()

    def copy(self, src, dst, device):
        i = self.used
        self.used += 1
        assert i < self.recv.shape[0]
        return Copy(self, lambda sem: pltpu.make_async_remote_copy(
            src_ref=src,
            dst_ref=dst,
            send_sem=sem,
            recv_sem=self.recv.at[i],
            device_id=device,
            device_id_type=MESH,
        ))

    def local(self, src, dst):
        return Copy(self, lambda sem: pltpu.make_async_copy(src, dst, sem))


N_SEND, N_SEND_Z = 44, 8
N_RECV, N_RECV_Z = 96, 10

AXES = {"d0": "xy", "d1": "yxz", "u0": "zxy", "u1": "zyx"}
DIRECT = ("p3",)
SCHEDULE = {
    "dk3": ("m",),
    "uk0": ("d0", "d0", "d1",),
    "uk1": ("d1",),
    "uk2": ("u0", "u1",),
    "uk3": ("u0", "u1",),
    "n1": ("d0",),
    "a0b": ("S", "O", "d1",),
    "a1a": ("u0", "d0", "p0", "m",),
    "a1w": ("S",),
    "a2a": ("p1", "u1",),
    "a2b": ("O",),
    "a3a": ("d0", "d1", "p2",),
    "a3w": ("S",),
    "sb": ("u0", "p1", "p0",),
    "end": (
        "u1", "p2", "O", "p3", "d1", "u1", "S", "p1", "u0", "S",
        "p0", "p2", "p3", "O", "p1", "d1", "p0", "O", "p2", "p1",
        "p0", "u1", "p2", "p3", "u0",
    ),
}


def kernel(
    cfg,
    series, cot_in, w_embed, w_q, w_k, w_v, w_o, w_up, w_down,
    b_embed, b_query, b_value, b_out, gain1, shift1, b_down, gain2, shift2, b_up,
    o_mixed, o_series, h_pairs, h_out, h_small, h_up, h_down,
    xs, xa, en, qkv, prob, ds, mxf, mx, rinv, inv1, flow, hid, slope, cot, g2, gb,
    qt, dt, wb, wqkv, wo, we, w2, ubb,
    g, rc, r1, r2, r3, rz,
    gp_, gprc, gpr1, gprz,
    go, gorc, gor1, gorz,
    gs, gsrc, gsr1, gsrz,
    o_pairs, o_out, o_small, o_up, o_down, vec, upv, ubl, send, recv,
):
    blocks, rows, padded, nz, fr = cfg
    n = blocks * padded
    look = we.shape[0]
    width = wo.shape[0]
    pairs = qkv.shape[0]
    hidden = w_up.shape[0]
    lanes2 = hidden // 2
    dp, t = lax.axis_index("dp"), lax.axis_index("tensor")
    c, y = t % 2, t // 2
    b, z = dp % 2, dp // 2
    co, yo, bo = 1 - c, 1 - y, 1 - b
    xy = y * 2 + b
    sems = Sems(send, recv)

    def dev(cc, yy, bb, zz=None):
        return ((z if zz is None else zz) * 2 + bb, yy * 2 + cc)

    core_dev, y_dev, x_dev = dev(co, y, b), dev(c, yo, b), dev(c, y, bo)
    xy_peers = [(y, bo), (yo, b), (yo, bo)]

    barrier = pltpu.get_barrier_semaphore()
    partners = [core_dev]
    partners += [dev(cc, py, pb) for cc in (c, co) for py, pb in xy_peers]
    partners += [dev(c, y, b, (z + k) % nz) for k in range(1, nz)]
    for partner in partners:
        pl.semaphore_signal(barrier, inc=1, device_id=partner, device_id_type=MESH)

    def load(src, dst):
        cp = sems.local(src, dst)
        cp.start()
        return cp

    load_vec = [load(b_up, upv)]
    for i, ref in enumerate(
        (b_embed, b_query, b_value, b_out, gain1, shift1, b_down, gain2, shift2)
    ):
        load_vec.append(load(ref, vec.at[i]))
    load_we = load(w_embed, we)
    load_qkv = []
    for p in range(pairs):
        for j, w in enumerate((w_q, w_k, w_v)):
            load_qkv.append(load(
                w.at[:, 128 * p:128 * p + 128], wqkv.at[p, :, 128 * j:128 * j + 128]
            ))
    own_x = load(series.at[t], xs.at[t, 0:look])
    own_w = [load(w, wb.at[m, t]) for m, w in enumerate((w_up, w_down))]
    load_wo = load(w_o, wo)
    own_cot = load(cot_in.at[t], cot.at[t])
    for cp in load_vec:
        cp.wait()
    ubl[...] = jnp.broadcast_to(upv[...].astype(F32).reshape(1, hidden), ubl.shape)
    ubb[t] = ubl[...]
    tail_rows = xs.shape[1] - look
    first = lax.broadcasted_iota(jnp.int32, (tail_rows, rows), 0) == 0
    for i in range(blocks):
        xs[i, look:, :] = jnp.where(first, 1.0, 0.0).astype(BF16)

    pl.semaphore_wait(barrier, len(partners))

    def exchange(src, dst, dst_at):
        out = []
        for k in range(1, blocks):
            other = (t + k) % blocks
            out.append(sems.copy(src.at[other], dst_at(dst), (dp, other)))
        return out

    send_x = exchange(series, xs, lambda r: r.at[t, 0:look])
    part = hidden // 4
    t_y, t_c, t_d = yo * 2 + c, y * 2 + co, yo * 2 + co
    stage_y, stage_core, stage_ub, stage_x, stage_d, stage_e = [], [], [], [], [], []
    for s in range(2):
        at = pl.ds(pl.multiple_of((b * 2 + s) * part, part), part)
        far = pl.ds(pl.multiple_of((bo * 2 + s) * part, part), part)
        for m, w in enumerate((w_up, w_down)):
            stage_y.append(sems.copy(w.at[at], wb.at[m, t, at], y_dev))
            stage_x.append(sems.copy(wb.at[m, t_y, at], wb.at[m, t_y, at], x_dev))
            stage_d.append(sems.copy(wb.at[m, t_y, at], wb.at[m, t_y, at], core_dev))
            stage_e.append(sems.copy(wb.at[m, t_y, far], wb.at[m, t_y, far], core_dev))
    for m, w in enumerate((w_up, w_down)):
        stage_core.append(sems.copy(w, wb.at[m, t], core_dev))
    for k in range(1, blocks):
        other = (t + k) % blocks
        stage_ub.append(sems.copy(ubl, ubb.at[t], (dp, other)))
    send_cot = exchange(cot_in, cot, lambda r: r.at[t])
    for cp in send_x + stage_ub + stage_y + stage_core + send_cot:
        cp.start()

    for cp in stage_x + stage_d + stage_e:
        cp.reserve()

    def forward_y(i):
        stage_y[i].wait_recv()
        stage_x[i].start()
        stage_d[i].start()

    def forward_x(i):
        stage_x[i].wait_recv()
        stage_e[i].start()

    load_we.wait()
    one_row = lax.broadcasted_iota(jnp.int32, (128, 1), 0)
    b_high = vec[EMBED].astype(BF16)
    b_low = vec[EMBED] - b_high.astype(F32)
    we_rows = pad_rows(we[...].astype(F32), 128)
    high = we_rows + jnp.where(one_row == look, b_high.astype(F32), 0.0)
    low = jnp.where(one_row == look, b_low, 0.0)
    w2[0, 0:128, :] = high.astype(BF16)
    w2[0, 128:256, :] = low.astype(BF16)
    both = (high + jnp.where(one_row == look + 1, b_low, 0.0)).astype(BF16)
    for cp in load_qkv:
        cp.wait()
    for p in range(pairs):
        at = slice(128 * p, 128 * p + 128)
        prod = mm(both, wqkv[p])
        bias = prod[look:look + 1] + prod[look + 1:look + 2]
        bias = bias + jnp.concatenate(
            [vec[QUERY, :, at], jnp.zeros((1, 128), F32), vec[VALUE, :, at]],
            axis=1,
        )
        prod = jnp.where(one_row < look, prod, jnp.where(one_row == look, bias, 0.0))
        factor = lax.broadcasted_iota(jnp.int32, (1, 384), 1)
        prod = prod * jnp.where(factor < 128, 0.125, 1.0)
        high = prod.astype(BF16)
        w2[1 + p, 0:128, 0:384] = high
        w2[1 + p, 128:256, 0:384] = (prod - high.astype(F32)).astype(BF16)
        qkv[p, :, 384:512] = jnp.ones((n, 128), BF16)

    own_x.wait()
    for cp in send_x:
        cp.wait()
    for i in range(blocks):
        x = pad_rows(xs[i].astype(F32).T, padded).astype(BF16)
        at = pl.ds(i * padded, padded)
        xa[at, 0:128] = x
        xa[at, 128:256] = x
    en[...] = mm(xa[...], w2[0])

    def project(p, carry):
        qkv[p, :, 0:384] = mm(xa[...], w2[1 + p, :, 0:384]).astype(BF16)
        return carry

    lax.fori_loop(0, pairs, project, 0)

    lane = lax.broadcasted_iota(jnp.int32, (1, 128), 1)
    key_at = lax.broadcasted_iota(jnp.int32, (1, n), 1)
    mask = jnp.where(key_at % padded >= rows, MASKED, 0.0).astype(F32)

    tile_f = 128

    def attend_pair(p, carry):
        for k in range(1, pairs):
            pl.when(p == k)(functools.partial(forward_y, k - 1))

        def attend_tile(i, carry):
            at = pl.ds(pl.multiple_of(i * tile_f, tile_f), tile_f)
            q = qkv[p, at, 0:128]
            outs, inverses = [], []
            for h in range(2):
                qm = jnp.where((lane // 64) == h, q, jnp.zeros_like(q))
                s = mm(qm, qkv[p, :, 128:256], 1, 1) + mask
                e = jnp.exp(s - jnp.max(s, axis=1, keepdims=True)).astype(BF16)
                prob[2 * p + h, at, :] = e
                o = mm(e, qkv[p, :, 256:512])
                outs.append(o[:, :128])
                inverses.append(1.0 / o[:, 128:])
            inverse = jnp.where(lane < 64, inverses[0], inverses[1])
            o = jnp.where(lane < 64, outs[0], outs[1]) * inverse
            lanes = pl.ds(pl.multiple_of(p * 128, 128), 128)
            mxf[at, lanes] = o
            mx[at, lanes] = o.astype(BF16)
            rinv[at, lanes] = inverse.astype(BF16)
            return carry

        lax.fori_loop(0, n // tile_f, attend_tile, 0, unroll=True)
        return carry

    lax.fori_loop(0, pairs, attend_pair, 0)
    forward_y(3)
    forward_x(0)
    forward_x(1)

    load_wo.wait()

    def first_norm(i, carry):
        at = pl.ds(pl.multiple_of(i * padded, padded), padded)
        zz = en[at, :] + (mm(mx[at, :], wo[...]) + vec[OUT])
        centred = zz - row_mean(zz)
        inv = lax.rsqrt(row_mean(centred * centred) + EPSILON)
        nn = centred * inv
        en[at, :] = nn
        inv1[at, :] = jnp.broadcast_to(inv, (padded, 128))
        out = nn * vec[GAIN1] + vec[SHIFT1]
        flow[at, :] = out.astype(BF16)
        g2[at, :] = out + vec[DOWN]
        return carry

    lax.fori_loop(0, blocks, first_norm, 0, unroll=True)
    forward_x(2)

    tile_h = n // 2

    def feed_forward(j):
        for i in range(n // tile_h):
            at = slice(i * tile_h, (i + 1) * tile_h)
            v = mm(flow[at, :], wb[0, j], 1, 1) + ubb[j, 0:1, :]
            v2 = v * v
            half = 0.5 * jnp.tanh(v * (GELU_A + GELU_B * v2)) + 0.5
            h = v * half
            slope[j, at, :] = (
                half + h * (1.0 - half) * (2 * GELU_A + (6 * GELU_B) * v2)
            ).astype(BF16)
            h = h.astype(BF16)
            hid[j, at, :] = h
            g2[at, :] += mm(h, wb[1, j])

    for cp in own_w:
        cp.wait()
    feed_forward(t)
    for cp in stage_core + stage_ub:
        cp.wait()
    feed_forward(t_c)
    forward_x(3)
    for cp in stage_x + stage_y:
        cp.wait_send()
    feed_forward(t_y)
    for cp in stage_d + stage_e:
        cp.wait()
    feed_forward(t_d)

    own_cot.wait()
    for cp in send_cot:
        cp.wait()

    def add_row(row, value, at=slice(None)):
        i = look + row
        gs[i // 64, (i // 16) % 4, i % 16:i % 16 + 1, at] += value

    gs[...] = jnp.zeros_like(gs)

    def second_norm(i, carry):
        at = pl.ds(pl.multiple_of(i * padded, padded), padded)
        acc = g2[at, :]
        centred = acc - row_mean(acc)
        inv = lax.rsqrt(row_mean(centred * centred) + EPSILON)
        nn = centred * inv
        up = pad_rows(cot[i].astype(F32), padded)
        result = nn * vec[GAIN2] + vec[SHIFT2]
        cot[i] = result[:rows].astype(BF16)
        gg = up * vec[GAIN2]
        back = inv * (gg - row_mean(gg) - nn * row_mean(gg * nn))
        g2[at, :] = back
        low = back.astype(BF16)
        gb[at, :] = low
        add_row(S_GAIN2, col_sum(up * nn))
        add_row(S_SHIFT2, col_sum(up))
        add_row(S_DOWN, col_sum(low.astype(F32)))
        return carry

    lax.fori_loop(0, blocks, second_norm, 0, unroll=True)
    own_mixed = sems.local(cot.at[t], o_mixed.at[t])
    own_mixed.start()
    send_mixed = [
        sems.copy(cot.at[other], o_mixed.at[t], (dp, other)) for other in (t_c, t_y, t_d)
    ]
    send_mixed[0].start()
    send_mixed_y = send_mixed[1:]

    def add_into(dst, src, index):
        dst[index] = (dst[index].astype(F32) + src[...].astype(F32)).astype(dst.dtype)

    results = []

    class Sum:
        def start(self, src, dst, device):
            cp = sems.copy(src, dst, device)
            cp.start()
            self.cps.append(cp)

        def wait(self):
            for cp in self.cps:
                cp.wait()
            self.cps = []

    def free_axes(order):
        axes = [a for a in order if a != "y"]
        return axes if "z" in axes else axes + ["z"]

    mine, theirs = {"x": b, "z": z % 2}, {"x": bo, "z": 1 - z % 2}
    z_near = z + 1 - 2 * (z % 2)
    axis_dev = {"y": y_dev, "x": x_dev, "z": dev(c, y, b, z_near)}

    class FeedSum(Sum):
        def __init__(self, m, h, axes, out):
            self.m, self.h, self.axes, self.out = m, h, axes, out
            self.free = free_axes(axes)
            self.core = []
            self.cps = []

        def at(self, *index):
            return (self.m, self.h) + index

        def send_core(self, k):
            cp = sems.copy(g.at[self.at(k)], rc.at[self.at(k)], core_dev)
            cp.start()
            self.core.append(cp)

        def add_core(self, k):
            self.core[k - 2].wait()
            add_into(g, rc.at[self.at(k - 2)], self.at(k))

        def send(self, axis, slices, fixed, to):
            for i, k in enumerate(slices):
                src = g.at[self.at(k, *fixed)]
                dst = to
                if axis != "y":
                    src = g.at[self.at(k, *fixed, theirs[axis])]
                    dst = to if len(slices) == 1 else to.at[i]
                self.start(src, dst, axis_dev[axis])

        def steps(self):
            m, h = self.m, self.h
            stages = [r1.at[m, h], r2.at[m, h], r3.at[m, h]]
            axes, fixed, slices = self.axes, [], [2, 3]
            self.add_core(2)
            if axes[0] == "y":
                self.send("y", [2], [], stages[0])
            else:
                self.start(
                    g.at[self.at(2, theirs[axes[0]])], stages[0].at[0], axis_dev[axes[0]]
                )
            yield
            self.add_core(3)
            if axes[0] != "y":
                self.start(
                    g.at[self.at(3, theirs[axes[0]])], stages[0].at[1], axis_dev[axes[0]]
                )
            yield
            for i, axis in enumerate(axes):
                self.wait()
                if axis == "y":
                    slices = [3]
                    add_into(g, stages[i], self.at(3, *fixed))
                else:
                    fixed = fixed + [mine[axis]]
                    for j, k in enumerate(slices):
                        got = stages[i] if len(slices) == 1 else stages[i].at[j]
                        add_into(g, got, self.at(k, *fixed))
                if i + 1 < len(axes):
                    nxt = axes[i + 1]
                    self.send(nxt, [2] if nxt == "y" else slices, fixed, stages[i + 1])
                    yield
            if "z" in axes:
                far = [((z // 2 + k) % (nz // 2)) for k in range(1, nz // 2)]
                parts = [(dev(c, y, b, f * 2 + z % 2), fixed + [f]) for f in far]
                own = fixed + [z // 2]
            else:
                far = [(z + k) % nz for k in range(1, nz)]
                parts = [(dev(c, y, b, f), fixed + [f % 2, f // 2]) for f in far]
                own = fixed + [z % 2, z // 2]
            for k, (to, at) in enumerate(parts):
                self.start(g.at[self.at(3, *at)], rz.at[m, h, k], to)
            yield
            self.wait()
            total = g[self.at(3, *own)].astype(F32)
            for k in range(len(parts)):
                total = total + rz[m, h, k].astype(F32)
            at = (slice(None), slice(h * lanes2, (h + 1) * lanes2))
            self.out[0][at] = total
            results.append(load(self.out[0].at[at], self.out[1].at[at]))

    class WholeSum(Sum):
        def __init__(self, key, grad, rcv, rcv1, rcvz, out, result):
            self.direct = key in DIRECT
            self.refs = (grad, rcv, rcv1, rcvz, out)
            self.result = result

        def steps(self):
            grad, rcv, rcv1, rcvz, out = self.refs
            self.cps = []
            if self.direct:
                for k, (py, pb) in enumerate([(y, b)] + xy_peers):
                    self.start(grad.at[co, py * 2 + pb], rcv.at[k], dev(co, py, pb))
            else:
                self.start(grad.at[co], rcv, core_dev)
                yield
                self.wait()
                for i in range(4):
                    add_into(grad, rcv.at[i], (c, i))
            for k, (py, pb) in enumerate(xy_peers):
                self.start(grad.at[c, py * 2 + pb], rcv1.at[k], dev(c, py, pb))
            yield
            self.wait()
            total = grad[c, xy].astype(F32)
            for k in range(3):
                total = total + rcv1[k].astype(F32)
            if self.direct:
                for k in range(4):
                    total = total + rcv[k].astype(F32)
            rcvz[z] = total.astype(grad.dtype)
            for k in range(1, nz):
                self.start(rcvz.at[z], rcvz.at[z], dev(c, y, b, (z + k) % nz))
            yield
            self.wait()
            total = rcvz[0].astype(F32)
            for k in range(1, nz):
                total = total + rcvz[k].astype(F32)
            out[c, xy] = total.astype(grad.dtype)
            for py, pb in xy_peers:
                self.start(out.at[c, xy], out.at[c, xy], dev(c, py, pb))
            if self.direct:
                for py, pb in [(y, b)] + xy_peers:
                    self.start(out.at[c, xy], out.at[c, xy], dev(co, py, pb))
            else:
                yield
                self.wait()
                self.start(out.at[c], out.at[c], core_dev)
            yield
            self.wait()
            results.append(load(out, self.result))

    chains = {}
    feeds = {}
    for m, (name, out) in enumerate((("d", (o_down, h_down)), ("u", (o_up, h_up)))):
        for h in range(2):
            key = name + str(h)
            feeds[key] = FeedSum(m, h, AXES[key], out)

    def point(name):
        for key in SCHEDULE.get(name, ()):
            if key == "m":
                send_mixed_y.pop(0).start()
            else:
                if key not in chains:
                    chains[key] = feeds[key].steps()
                next(chains[key], None)

    order = (t_d, t_c, t_y, t)

    def feed_grad(m, k, left, right):
        out = mm(left, right, 0, 0).astype(BF16)
        for h in range(2):
            for zz in range(nz):
                for bb in range(2):
                    i = (zz * 2 + bb) * fr
                    at = {"x": bb, "z": zz % 2}
                    at = tuple(at[a] for a in feeds["du"[m] + str(h)].free)
                    g[(m, h, k) + at + (zz // 2,)] = out[i:i + fr, h * lanes2:(h + 1) * lanes2]

    point("n2")

    for k, j in enumerate(order):
        feed_grad(0, k, gb[...], hid[j])
        if k < 2:
            feeds["d0"].send_core(k)
            feeds["d1"].send_core(k)
        point("dk" + str(k))

    def feed_back(k, j):
        for i in range(n // tile_h):
            at = slice(i * tile_h, (i + 1) * tile_h)
            gp = (slope[j, at, :].astype(F32) * mm(gb[at, :], wb[1, j], 1, 1)).astype(BF16)
            slope[j, at, :] = gp
            g2[at, :] += mm(gp, wb[0, j])
        up_rows[k] = col_sum(slope[j].astype(F32))
        feed_grad(1, k, flow[...], slope[j])

    up_rows = [None] * blocks
    for k, j in enumerate(order):
        feed_back(k, j)
        if k < 2:
            feeds["u0"].send_core(k)
            feeds["u1"].send_core(k)
        point("uk" + str(k))
    for k, j in enumerate(order):
        i = look + S_UP + j
        gs[i // 64, (i // 16) % 4, pl.ds(i % 16, 1), :] = up_rows[k]

    def first_back(i, carry):
        at = pl.ds(pl.multiple_of(i * padded, padded), padded)
        acc = g2[at, :]
        nn = en[at, :]
        add_row(S_GAIN1, col_sum(acc * nn))
        add_row(S_SHIFT1, col_sum(acc))
        gg = acc * vec[GAIN1]
        inv = inv1[at, 0:1]
        back = inv * (gg - row_mean(gg) - nn * row_mean(gg * nn))
        ga = back.astype(BF16)
        hid[0, at, :] = ga
        gm = mm(ga, wo[...], 1, 1)
        gb[at, :] = (gm * rinv[at, :].astype(F32)).astype(BF16)
        return carry

    lax.fori_loop(0, blocks, first_back, 0, unroll=True)
    point("n1")

    ga = hid.at[0]
    out_grad = mm(mx[...], ga[...], 0, 0).astype(BF16)
    for i in range(8):
        r = width // 8
        go[i // 4, i % 4] = out_grad[i * r:(i + 1) * r]
    chains["O"] = WholeSum("O", go, gorc, gor1, gorz, o_out, h_out).steps()
    next(chains["O"])
    small = mm(xa[:, 0:128], ga[...], 0, 0)
    for i in range(8):
        gs[i // 4, i % 4] += small[16 * i:16 * i + 16]
    chains["S"] = WholeSum("S", gs, gsrc, gsr1, gsrz, o_small, h_small).steps()
    next(chains["S"])
    point("og")

    tile_b = n // 2

    def attend_back(p):
        lanes = pl.ds(p * 128, 128)
        qt[...] = qkv[p, :, 0:128].T
        dt[...] = gb[:, lanes].T
        for h in range(2):
            def tile(i, carry):
                at = pl.ds(pl.multiple_of(i * tile_b, tile_b), tile_b)
                d = gb[at, lanes]
                own = (lane // 64) == h
                dm = jnp.where(own, d, jnp.zeros_like(d))
                centre = jnp.sum(
                    jnp.where(own, d.astype(F32) * mxf[at, lanes], 0.0), axis=1, keepdims=True
                )
                s = (mm(dm, qkv[p, :, 256:384], 1, 1) - centre).astype(BF16)
                s = s * prob[2 * p + h, at, :]
                ds[at, :] = s
                dq = mm(s, qkv[p, :, 128:256])
                if h == 0:
                    mxf[at, lanes] = jnp.where(lane < 64, dq, mxf[at, lanes])
                else:
                    rinv[at, lanes] = jnp.where(lane < 64, mxf[at, lanes], dq).astype(BF16)
                return carry

            lax.fori_loop(0, n // tile_b, tile, 0, unroll=True)
            half = slice(64 * h, 64 * h + 64)
            dk = mm(qt[half, :], ds[...])
            dv = mm(dt[half, :], prob[2 * p + h])
            qt[half, :] = dk.astype(BF16)
            dt[half, :] = dv.astype(BF16)
            point("a" + str(p) + "ab"[h])
        qkv[p, :, 0:128] = rinv[:, lanes]
        qkv[p, :, 128:256] = qt[...].T
        qkv[p, :, 256:384] = dt[...].T
        grad = mm(xa[:, 0:128], qkv[p, :, 0:384], 0, 0).astype(BF16)
        for i in range(8):
            gp_[p, i // 4, i % 4] = grad[16 * i:16 * i + 16]
        key = "p" + str(p)
        chains[key] = WholeSum(
            key, gp_.at[p], gprc.at[p], gpr1.at[p], gprz.at[p], o_pairs.at[p], h_pairs.at[p]
        ).steps()
        next(chains[key])
        point("a" + str(p) + "w")

    attend_back(0)
    attend_back(1)
    attend_back(2)
    attend_back(3)

    out = mm(we[...], ga[...], 1, 1)
    for p in range(pairs):
        out = out + mm(w2[1 + p, 0:look, 0:384], qkv[p, :, 0:384], 1, 1)
    for i in range(blocks):
        xs[i, 0:look, :] = out[:, i * padded:i * padded + rows].astype(BF16)
    own_s = sems.local(xs.at[t, 0:look], o_series.at[t])
    own_s.start()
    send_s = []
    for k in range(1, blocks):
        other = (t + k) % blocks
        send_s.append(sems.copy(xs.at[other, 0:look], o_series.at[t], (dp, other)))
    for cp in send_s:
        cp.start()
    point("sb")
    point("end")
    while send_mixed_y:
        send_mixed_y.pop(0).start()
    for _ in range(6):
        for key in chains:
            next(chains[key], None)
    for cp in send_s + send_mixed:
        cp.wait()
    for cp in results + [own_s, own_mixed]:
        cp.wait()


def finish(cfg, *refs):
    pairs, n_in, n_out = cfg
    inputs, refs = refs[:n_in], refs[n_in:]
    results, refs = refs[:n_out], refs[n_out:]
    held, refs = refs[:n_in], refs[n_in:]
    made, (sem_in, sem_out) = refs[:-2], refs[-2:]
    mixed, sgrad, up, down, pair_sums, out, small, we, wq, wk, wv, be = held
    made = (mixed, sgrad, up, down) + tuple(made)
    loads = [
        pltpu.make_async_copy(src, dst, sem_in.at[i])
        for i, (src, dst) in enumerate(zip(inputs, held))
    ]
    stores = [
        pltpu.make_async_copy(src, dst, sem_out.at[i])
        for i, (src, dst) in enumerate(zip(made, results))
    ]
    o_q, o_k, o_v, o_o, o_we, o_be, o_bq, o_bv, o_bo, o_g1, o_s1, o_bu, o_bd, o_g2, o_s2 = made[4:]
    for i in (4, 7, 11, 8, 9, 10, 6, 5, 0, 1, 2, 3):
        loads[i].start()
    look, width = we.shape
    r = width // 8
    for i in (4, 7, 11):
        loads[i].wait()
    row = lax.broadcasted_iota(jnp.int32, (128, 1), 0)
    b_high = be[...].astype(BF16).astype(F32)
    left = pad_rows(we[...].astype(F32), 128)
    left = left + jnp.where(row == look, b_high, 0.0)
    left = (left + jnp.where(row == look + 1, be[...] - b_high, 0.0)).astype(BF16)
    total = jnp.zeros((128, width), F32)
    for j, (o, w) in enumerate(((o_q, wq), (o_k, wk), (o_v, wv))):
        sums = jnp.concatenate(
            [
                jnp.concatenate(
                    [pair_sums[p, i // 4, i % 4, :, 128 * j:128 * j + 128] for i in range(8)],
                    axis=0,
                ).astype(F32)
                for p in range(pairs)
            ],
            axis=1,
        )
        if j == 0:
            sums = sums * 0.125
        last = sums[look:look + 1]
        o[...] = mm(left, (sums + jnp.where(row == look + 1, last, 0.0)).astype(BF16), 0, 0)
        stores[4 + j].start()
        if j == 0:
            o_bq[...] = last
        if j == 2:
            o_bv[...] = last
        loads[8 + j].wait()
        total = total + mm(sums.astype(BF16), w[...], 1, 1)
    loads[6].wait()
    total = total + jnp.concatenate([small[i // 4, i % 4] for i in range(8)], axis=0)
    o_we[...] = total[:look]
    o_be[...] = total[look:look + 1]

    def vector(i):
        i = look + i
        return small[i // 64, (i // 16) % 4, i % 16:i % 16 + 1, :]

    o_bo[...] = vector(0)
    for o, i in (
        (o_g1, S_GAIN1), (o_s1, S_SHIFT1), (o_bd, S_DOWN), (o_g2, S_GAIN2), (o_s2, S_SHIFT2)
    ):
        o[...] = vector(i)
    for i in range(4):
        o_bu[:, i * width:(i + 1) * width] = vector(S_UP + i)
    for cp in stores[8:]:
        cp.start()
    loads[5].wait()
    for i in range(8):
        o_o[i * r:(i + 1) * r, :] = out[i // 4, i % 4].astype(F32)
    stores[7].start()
    for i in range(4):
        loads[i].wait()
        stores[i].start()
    for cp in stores:
        cp.wait()


def body(
    series, embed_weight, embed_bias, query_weight, query_bias, key_weight, value_weight,
    value_bias, out_weight, out_bias, first_gain, first_shift, up_weight, up_bias,
    down_weight, down_bias, second_gain, second_shift, cotangent,
    *, dp_size, tensor_size,
):
    windows, rows, look = series.shape
    width = embed_weight.shape[1]
    hidden = up_weight.shape[0]
    pairs = HEADS // 2
    assert windows == tensor_size == 4 and width == hidden == HEADS * 64
    assert dp_size % 4 == 0 and look % 16 == 0 and look + S_UP + 4 <= 128
    padded = -(-rows // 32) * 32
    n = tensor_size * padded
    nz = dp_size // 2
    fr = width // dp_size
    r = width // 8
    half = hidden // 2

    def scr(*shape, dtype=BF16):
        return pltpu.VMEM(shape, dtype)

    scratch = [
        scr(4, 128, rows),
        scr(n, 256),
        scr(n, width, dtype=F32),
        scr(pairs, n, 512),
        scr(HEADS, n, n),
        scr(n, n),
        scr(n, width, dtype=F32),
        scr(n, width),
        scr(n, width),
        scr(n, 128, dtype=F32),
        scr(n, width),
        scr(4, n, hidden),
        scr(4, n, hidden),
        scr(4, rows, width),
        scr(n, width, dtype=F32),
        scr(n, width),
        scr(128, n),
        scr(128, n),
        scr(2, 4, hidden, width),
        scr(pairs, width, 384),
        scr(width, width),
        scr(look, width),
        scr(1 + pairs, 256, width),
        scr(4, 8, hidden, dtype=F32),
        scr(2, 2, 4, 2, 2, nz // 2, fr, half),
        scr(2, 2, 2, 2, 2, nz // 2, fr, half),
        scr(2, 2, 2, 2, nz // 2, fr, half),
        scr(2, 2, 2, nz // 2, fr, half),
        scr(2, 2, nz // 2, fr, half),
        scr(2, 2, nz - 1, fr, half),
        scr(pairs, 2, 4, 16, 384),
        scr(pairs, 4, 16, 384),
        scr(pairs, 3, 16, 384),
        scr(pairs, nz, 16, 384),
        scr(2, 4, r, width),
        scr(4, r, width),
        scr(3, r, width),
        scr(nz, r, width),
        scr(2, 4, 16, width, dtype=F32),
        scr(4, 16, width, dtype=F32),
        scr(3, 16, width, dtype=F32),
        scr(nz, 16, width, dtype=F32),
        scr(pairs, 2, 4, 16, 384),
        scr(2, 4, r, width),
        scr(2, 4, 16, width, dtype=F32),
        scr(fr, hidden, dtype=F32),
        scr(fr, hidden, dtype=F32),
        scr(9, 1, width, dtype=F32),
        scr(hidden),
        scr(8, hidden, dtype=F32),
        pltpu.SemaphoreType.DMA((N_SEND + N_SEND_Z * nz,)),
        pltpu.SemaphoreType.DMA((N_RECV + N_RECV_Z * nz,)),
    ]
    hbm = pl.BlockSpec(memory_space=pl.ANY)
    vmem = pl.BlockSpec(memory_space=pltpu.VMEM)
    sd = jax.ShapeDtypeStruct
    bias = embed_bias.reshape(1, -1)
    mixed, sgrad, g_pairs, g_out, g_small, g_up, g_down = pl.pallas_call(
        functools.partial(kernel, (4, rows, padded, nz, fr)),
        out_shape=[
            sd((4, rows, width), BF16),
            sd((4, look, rows), BF16),
            sd((pairs, 2, 4, 16, 384), BF16),
            sd((2, 4, r, width), BF16),
            sd((2, 4, 16, width), F32),
            sd((fr, hidden), F32),
            sd((fr, hidden), F32),
        ],
        in_specs=[hbm] * 19,
        out_specs=[hbm] * 7,
        scratch_shapes=scratch,
        compiler_params=pltpu.CompilerParams(
            collective_id=1, has_side_effects=True, vmem_limit_bytes=64 * 1024 * 1024
        ),
    )(
        jnp.swapaxes(series, 1, 2), cotangent, embed_weight, query_weight, key_weight,
        value_weight, out_weight, up_weight, down_weight, bias,
        *(v.reshape(1, -1) for v in (
            query_bias, value_bias, out_bias, first_gain, first_shift, down_bias,
            second_gain, second_shift,
        )),
        up_bias,
    )
    vector = sd((1, width), F32)
    operands = (
        mixed, sgrad, g_up, g_down, g_pairs, g_out, g_small, embed_weight, query_weight,
        key_weight, value_weight, bias,
    )
    made = [
        *[sd((width, width), F32)] * 4,
        sd((look, width), F32),
        *[vector] * 6,
        sd((1, 4 * hidden), F32),
        *[vector] * 3,
    ]
    out = pl.pallas_call(
        functools.partial(finish, (pairs, len(operands), 4 + len(made))),
        out_shape=[sd(a.shape, a.dtype) for a in operands[:4]] + made,
        in_specs=[hbm] * len(operands),
        out_specs=[hbm] * (4 + len(made)),
        scratch_shapes=[
            *[scr(*a.shape, dtype=a.dtype) for a in operands],
            *[scr(*a.shape, dtype=a.dtype) for a in made],
            pltpu.SemaphoreType.DMA((len(operands),)),
            pltpu.SemaphoreType.DMA((4 + len(made),)),
        ],
        compiler_params=pltpu.CompilerParams(vmem_limit_bytes=64 * 1024 * 1024),
    )(*operands)
    mixed, sgrad, g_up, g_down, g_q, g_k, g_v, g_o, g_e = out[:9]
    g_be, g_bq, g_bv, g_bo, g_g1, g_s1, g_bu, g_bd, g_g2, g_s2 = (
        v.reshape(-1) for v in out[9:]
    )
    return (
        mixed, jnp.swapaxes(sgrad, 1, 2), g_e, g_be, g_q, g_bq, g_k, g_v, g_bv, g_o, g_bo,
        g_g1, g_s1, g_up.T, g_bu, g_down.T, g_bd, g_g2, g_s2,
    )


def solution(mesh):
    token = P("dp", "tensor", None)
    return jax.shard_map(
        functools.partial(
            body, dp_size=mesh.shape["dp"], tensor_size=mesh.shape["tensor"]
        ),
        mesh=mesh,
        in_specs=(
            token, P(), P(), P(), P(), P(), P(), P(), P(), P(), P(), P(),
            P("tensor", None), P("tensor"), P("tensor", None), P(), P(), P(), token,
        ),
        out_specs=(
            token, token, P(), P(), P(), P(), P(), P(), P(), P(), P(), P(), P(),
            P("tensor", "dp"), P(), P("tensor", "dp"), P(), P(), P(),
        ),
        check_vma=False,
    )
```

```python
import functools
import jax
import jax.numpy as jnp
from jax import lax
from jax.experimental import pallas as pl
from jax.experimental.pallas import tpu as pltpu
from jax.sharding import PartitionSpec as P

HEADS = 8
EPSILON = 1e-05
F32 = jnp.float32
BF16 = jnp.bfloat16
MESH = pl.DeviceIdType.MESH
GELU_A = 0.7978845608028654
GELU_B = GELU_A * 0.044715
MASKED = -1e30

EMBED, QUERY, VALUE, OUT, GAIN1, SHIFT1, DOWN, GAIN2, SHIFT2 = range(9)
S_GAIN1, S_SHIFT1, S_DOWN, S_GAIN2, S_SHIFT2, S_UP = range(1, 7)


def mm(left, right, cl=1, cr=0):
    return lax.dot_general(
        left, right, (((cl,), (cr,)), ((), ())), preferred_element_type=F32
    )


def row_mean(x):
    return jnp.mean(x, axis=1, keepdims=True)


def col_sum(x):
    return jnp.sum(x, axis=0, keepdims=True)


def pad_rows(x, rows):
    if x.shape[0] == rows:
        return x
    return jnp.concatenate([x, jnp.zeros((rows - x.shape[0], x.shape[1]), x.dtype)], axis=0)


class Copy:
    def __init__(self, sems, make):
        self.sems, self.make, self.copy = sems, make, None

    def reserve(self):
        self.slot = self.sems.take()
        self.copy = self.make(self.sems.send.at[self.slot])

    def start(self):
        if self.copy is None:
            self.reserve()
        self.copy.start()

    def wait_recv(self):
        self.copy.wait_recv()

    def wait_send(self):
        self.copy.wait_send()
        self.sems.free.append(self.slot)

    def wait(self):
        self.copy.wait()
        self.sems.free.append(self.slot)


class Sems:
    def __init__(self, send, recv):
        self.send, self.recv = send, recv
        self.free = list(range(send.shape[0]))[::-1]
        self.used = 0

    def take(self):
        return self.free.pop()

    def copy(self, src, dst, device):
        i = self.used
        self.used += 1
        assert i < self.recv.shape[0]
        return Copy(self, lambda sem: pltpu.make_async_remote_copy(
            src_ref=src,
            dst_ref=dst,
            send_sem=sem,
            recv_sem=self.recv.at[i],
            device_id=device,
            device_id_type=MESH,
        ))

    def local(self, src, dst):
        return Copy(self, lambda sem: pltpu.make_async_copy(src, dst, sem))


N_SEND, N_SEND_Z = 30, 5
N_RECV, N_RECV_Z = 94, 10

AXES = {"d0": "xy", "d1": "yxz", "u0": "zxy", "u1": "zyx"}
DIRECT = ("p3",)
SCHEDULE = {
    "dk3": ("m",),
    "uk0": ("d0", "d0", "d1",),
    "uk1": ("d1",),
    "uk2": ("u0", "u1",),
    "uk3": ("u0", "u1",),
    "n1": ("d0",),
    "a0b": ("S", "O", "d1",),
    "a1a": ("u0", "d0", "p0", "m",),
    "a1w": ("S",),
    "a2a": ("p1", "u1",),
    "a2b": ("O",),
    "a3a": ("d0", "d1", "p2",),
    "a3w": ("S",),
    "sb": ("u0", "p1", "p0",),
    "end": (
        "u1", "p2", "O", "p3", "d1", "u1", "S", "p1", "u0", "S",
        "p0", "p2", "p3", "O", "p1", "d1", "p0", "O", "p2", "p1",
        "p0", "u1", "p2", "p3", "u0",
    ),
}


def kernel(
    cfg,
    series, cot_in, w_embed, w_q, w_k, w_v, w_o, w_up, w_down,
    b_embed, b_query, b_value, b_out, gain1, shift1, b_down, gain2, shift2, b_up,
    o_mixed, o_series, h_pairs, h_out, h_small, h_up, h_down,
    xs, xa, en, qkv, prob, ds, mxf, mx, rinv, inv1, flow, hid, slope, cot, g2, gb,
    qt, dt, wb, wqkv, wo, we, w2, ubb,
    g, rc, r1, r2, r3, rz,
    gp_, gprc, gpr1, gprz,
    go, gorc, gor1, gorz,
    gs, gsrc, gsr1, gsrz,
    o_pairs, o_out, o_small, o_up, o_down, vec, upv, ubl, send, recv,
):
    blocks, rows, padded, nz, fr = cfg
    n = blocks * padded
    look = we.shape[0]
    width = wo.shape[0]
    pairs = qkv.shape[0]
    hidden = w_up.shape[0]
    lanes2 = hidden // 2
    dp, t = lax.axis_index("dp"), lax.axis_index("tensor")
    c, y = t % 2, t // 2
    b, z = dp % 2, dp // 2
    co, yo, bo = 1 - c, 1 - y, 1 - b
    xy = y * 2 + b
    sems = Sems(send, recv)

    def dev(cc, yy, bb, zz=None):
        return ((z if zz is None else zz) * 2 + bb, yy * 2 + cc)

    core_dev, y_dev, x_dev = dev(co, y, b), dev(c, yo, b), dev(c, y, bo)
    xy_peers = [(y, bo), (yo, b), (yo, bo)]

    barrier = pltpu.get_barrier_semaphore()
    partners = [core_dev]
    partners += [dev(cc, py, pb) for cc in (c, co) for py, pb in xy_peers]
    partners += [dev(c, y, b, (z + k) % nz) for k in range(1, nz)]
    for partner in partners:
        pl.semaphore_signal(barrier, inc=1, device_id=partner, device_id_type=MESH)

    def load(src, dst):
        cp = sems.local(src, dst)
        cp.start()
        return cp

    load_vec = [load(b_up, upv)]
    for i, ref in enumerate(
        (b_embed, b_query, b_value, b_out, gain1, shift1, b_down, gain2, shift2)
    ):
        load_vec.append(load(ref, vec.at[i]))
    load_we = load(w_embed, we)
    load_qkv = []
    for p in range(pairs):
        for j, w in enumerate((w_q, w_k, w_v)):
            load_qkv.append(load(
                w.at[:, 128 * p:128 * p + 128], wqkv.at[p, :, 128 * j:128 * j + 128]
            ))
    own_x = load(series.at[t], xs.at[t, 0:look])
    own_w = [load(w, wb.at[m, t]) for m, w in enumerate((w_up, w_down))]
    load_wo = load(w_o, wo)
    own_cot = load(cot_in.at[t], cot.at[t])
    for cp in load_vec:
        cp.wait()
    ubl[...] = jnp.broadcast_to(upv[...].astype(F32), ubl.shape)
    ubb[t] = ubl[...]
    tail_rows = xs.shape[1] - look
    first = lax.broadcasted_iota(jnp.int32, (tail_rows, rows), 0) == 0
    for i in range(blocks):
        xs[i, look:, :] = jnp.where(first, 1.0, 0.0).astype(BF16)

    pl.semaphore_wait(barrier, len(partners))

    def exchange(src, dst, dst_at):
        out = []
        for k in range(1, blocks):
            other = (t + k) % blocks
            out.append(sems.copy(src.at[other], dst_at(dst), (dp, other)))
        return out

    send_x = exchange(series, xs, lambda r: r.at[t, 0:look])
    part = hidden // 4
    t_y, t_c, t_d = yo * 2 + c, y * 2 + co, yo * 2 + co
    stage_y, stage_core, stage_ub, stage_x, stage_d, stage_e = [], [], [], [], [], []
    for s in range(2):
        at = pl.ds(pl.multiple_of((b * 2 + s) * part, part), part)
        far = pl.ds(pl.multiple_of((bo * 2 + s) * part, part), part)
        for m, w in enumerate((w_up, w_down)):
            stage_y.append(sems.copy(w.at[at], wb.at[m, t, at], y_dev))
            stage_x.append(sems.copy(wb.at[m, t_y, at], wb.at[m, t_y, at], x_dev))
            stage_d.append(sems.copy(wb.at[m, t_y, at], wb.at[m, t_y, at], core_dev))
            stage_e.append(sems.copy(wb.at[m, t_y, far], wb.at[m, t_y, far], core_dev))
    for m, w in enumerate((w_up, w_down)):
        stage_core.append(sems.copy(w, wb.at[m, t], core_dev))
    for k in range(1, blocks):
        other = (t + k) % blocks
        stage_ub.append(sems.copy(ubl, ubb.at[t], (dp, other)))
    send_cot = exchange(cot_in, cot, lambda r: r.at[t])
    for cp in send_x + stage_ub + stage_y + stage_core + send_cot:
        cp.start()

    for cp in stage_x + stage_d + stage_e:
        cp.reserve()

    def forward_y(i):
        stage_y[i].wait_recv()
        stage_x[i].start()
        stage_d[i].start()

    def forward_x(i):
        stage_x[i].wait_recv()
        stage_e[i].start()

    load_we.wait()
    one_row = lax.broadcasted_iota(jnp.int32, (128, 1), 0)
    b_high = vec[EMBED].astype(BF16)
    b_low = vec[EMBED] - b_high.astype(F32)
    we_rows = pad_rows(we[...].astype(F32), 128)
    high = we_rows + jnp.where(one_row == look, b_high.astype(F32), 0.0)
    low = jnp.where(one_row == look, b_low, 0.0)
    w2[0, 0:128, :] = high.astype(BF16)
    w2[0, 128:256, :] = low.astype(BF16)
    both = (high + jnp.where(one_row == look + 1, b_low, 0.0)).astype(BF16)
    for cp in load_qkv:
        cp.wait()
    for p in range(pairs):
        at = slice(128 * p, 128 * p + 128)
        prod = mm(both, wqkv[p])
        bias = prod[look:look + 1] + prod[look + 1:look + 2]
        bias = bias + jnp.concatenate(
            [vec[QUERY, :, at], jnp.zeros((1, 128), F32), vec[VALUE, :, at]],
            axis=1,
        )
        prod = jnp.where(one_row < look, prod, jnp.where(one_row == look, bias, 0.0))
        factor = lax.broadcasted_iota(jnp.int32, (1, 384), 1)
        prod = prod * jnp.where(factor < 128, 0.125, 1.0)
        high = prod.astype(BF16)
        w2[1 + p, 0:128, 0:384] = high
        w2[1 + p, 128:256, 0:384] = (prod - high.astype(F32)).astype(BF16)
        qkv[p, :, 384:512] = jnp.ones((n, 128), BF16)

    own_x.wait()
    for cp in send_x:
        cp.wait()
    for i in range(blocks):
        x = pad_rows(xs[i].astype(F32).T, padded).astype(BF16)
        at = pl.ds(i * padded, padded)
        xa[at, 0:128] = x
        xa[at, 128:256] = x
    en[...] = mm(xa[...], w2[0])

    def project(p, carry):
        qkv[p, :, 0:384] = mm(xa[...], w2[1 + p, :, 0:384]).astype(BF16)
        return carry

    lax.fori_loop(0, pairs, project, 0)

    lane = lax.broadcasted_iota(jnp.int32, (1, 128), 1)
    key_at = lax.broadcasted_iota(jnp.int32, (1, n), 1)
    mask = jnp.where(key_at % padded >= rows, MASKED, 0.0).astype(F32)

    tile_f = 128

    def attend_pair(p, carry):
        for k in range(1, pairs):
            pl.when(p == k)(functools.partial(forward_y, k - 1))

        def attend_tile(i, carry):
            at = pl.ds(pl.multiple_of(i * tile_f, tile_f), tile_f)
            q = qkv[p, at, 0:128]
            outs, inverses = [], []
            for h in range(2):
                qm = jnp.where((lane // 64) == h, q, jnp.zeros_like(q))
                s = mm(qm, qkv[p, :, 128:256], 1, 1) + mask
                e = jnp.exp(s - jnp.max(s, axis=1, keepdims=True)).astype(BF16)
                prob[2 * p + h, at, :] = e
                o = mm(e, qkv[p, :, 256:512])
                outs.append(o[:, :128])
                inverses.append(1.0 / o[:, 128:])
            inverse = jnp.where(lane < 64, inverses[0], inverses[1])
            o = jnp.where(lane < 64, outs[0], outs[1]) * inverse
            lanes = pl.ds(pl.multiple_of(p * 128, 128), 128)
            mxf[at, lanes] = o
            mx[at, lanes] = o.astype(BF16)
            rinv[at, lanes] = inverse.astype(BF16)
            return carry

        lax.fori_loop(0, n // tile_f, attend_tile, 0, unroll=True)
        return carry

    lax.fori_loop(0, pairs, attend_pair, 0)
    forward_y(3)
    forward_x(0)
    forward_x(1)

    load_wo.wait()

    def first_norm(i, carry):
        at = pl.ds(pl.multiple_of(i * padded, padded), padded)
        zz = en[at, :] + (mm(mx[at, :], wo[...]) + vec[OUT])
        centred = zz - row_mean(zz)
        inv = lax.rsqrt(row_mean(centred * centred) + EPSILON)
        nn = centred * inv
        en[at, :] = nn
        inv1[at, :] = jnp.broadcast_to(inv, (padded, 128))
        out = nn * vec[GAIN1] + vec[SHIFT1]
        flow[at, :] = out.astype(BF16)
        g2[at, :] = out + vec[DOWN]
        return carry

    lax.fori_loop(0, blocks, first_norm, 0, unroll=True)
    forward_x(2)

    tile_h = n // 2

    def feed_forward(j):
        for i in range(n // tile_h):
            at = slice(i * tile_h, (i + 1) * tile_h)
            v = mm(flow[at, :], wb[0, j], 1, 1) + ubb[j, 0:1, :]
            v2 = v * v
            half = 0.5 * jnp.tanh(v * (GELU_A + GELU_B * v2)) + 0.5
            h = v * half
            slope[j, at, :] = (
                half + h * (1.0 - half) * (2 * GELU_A + (6 * GELU_B) * v2)
            ).astype(BF16)
            h = h.astype(BF16)
            hid[j, at, :] = h
            g2[at, :] += mm(h, wb[1, j])

    for cp in own_w:
        cp.wait()
    feed_forward(t)
    for cp in stage_core + stage_ub:
        cp.wait()
    feed_forward(t_c)
    forward_x(3)
    for cp in stage_x + stage_y:
        cp.wait_send()
    feed_forward(t_y)
    for cp in stage_d + stage_e:
        cp.wait()
    feed_forward(t_d)

    own_cot.wait()
    for cp in send_cot:
        cp.wait()

    def add_row(row, value, at=slice(None)):
        i = look + row
        gs[i // 64, (i // 16) % 4, i % 16:i % 16 + 1, at] += value

    gs[...] = jnp.zeros_like(gs)

    def second_norm(i, carry):
        at = pl.ds(pl.multiple_of(i * padded, padded), padded)
        acc = g2[at, :]
        centred = acc - row_mean(acc)
        inv = lax.rsqrt(row_mean(centred * centred) + EPSILON)
        nn = centred * inv
        up = pad_rows(cot[i].astype(F32), padded)
        result = nn * vec[GAIN2] + vec[SHIFT2]
        cot[i] = result[:rows].astype(BF16)
        gg = up * vec[GAIN2]
        back = inv * (gg - row_mean(gg) - nn * row_mean(gg * nn))
        g2[at, :] = back
        low = back.astype(BF16)
        gb[at, :] = low
        add_row(S_GAIN2, col_sum(up * nn))
        add_row(S_SHIFT2, col_sum(up))
        add_row(S_DOWN, col_sum(low.astype(F32)))
        return carry

    lax.fori_loop(0, blocks, second_norm, 0, unroll=True)
    own_mixed = sems.local(cot.at[t], o_mixed.at[t])
    own_mixed.start()
    send_mixed = [
        sems.copy(cot.at[other], o_mixed.at[t], (dp, other)) for other in (t_c, t_y, t_d)
    ]
    send_mixed[0].start()
    send_mixed_y = send_mixed[1:]

    def add_into(dst, src, index):
        dst[index] = (dst[index].astype(F32) + src[...].astype(F32)).astype(dst.dtype)

    results = []

    class Sum:
        def start(self, src, dst, device):
            cp = sems.copy(src, dst, device)
            cp.start()
            self.cps.append(cp)

        def wait(self):
            for cp in self.cps:
                cp.wait()
            self.cps = []

    def free_axes(order):
        axes = [a for a in order if a != "y"]
        return axes if "z" in axes else axes + ["z"]

    mine, theirs = {"x": b, "z": z % 2}, {"x": bo, "z": 1 - z % 2}
    z_near = z + 1 - 2 * (z % 2)
    axis_dev = {"y": y_dev, "x": x_dev, "z": dev(c, y, b, z_near)}

    class FeedSum(Sum):
        def __init__(self, m, h, axes, out):
            self.m, self.h, self.axes, self.out = m, h, axes, out
            self.free = free_axes(axes)
            self.core = []
            self.cps = []

        def at(self, *index):
            return (self.m, self.h) + index

        def send_core(self, k):
            cp = sems.copy(g.at[self.at(k)], rc.at[self.at(k)], core_dev)
            cp.start()
            self.core.append(cp)

        def add_core(self, k):
            self.core[k - 2].wait()
            add_into(g, rc.at[self.at(k - 2)], self.at(k))

        def send(self, axis, slices, fixed, to):
            for i, k in enumerate(slices):
                src = g.at[self.at(k, *fixed)]
                dst = to
                if axis != "y":
                    src = g.at[self.at(k, *fixed, theirs[axis])]
                    dst = to if len(slices) == 1 else to.at[i]
                self.start(src, dst, axis_dev[axis])

        def steps(self):
            m, h = self.m, self.h
            stages = [r1.at[m, h], r2.at[m, h], r3.at[m, h]]
            axes, fixed, slices = self.axes, [], [2, 3]
            self.add_core(2)
            if axes[0] == "y":
                self.send("y", [2], [], stages[0])
            else:
                self.start(
                    g.at[self.at(2, theirs[axes[0]])], stages[0].at[0], axis_dev[axes[0]]
                )
            yield
            self.add_core(3)
            if axes[0] != "y":
                self.start(
                    g.at[self.at(3, theirs[axes[0]])], stages[0].at[1], axis_dev[axes[0]]
                )
            yield
            for i, axis in enumerate(axes):
                self.wait()
                if axis == "y":
                    slices = [3]
                    add_into(g, stages[i], self.at(3, *fixed))
                else:
                    fixed = fixed + [mine[axis]]
                    for j, k in enumerate(slices):
                        got = stages[i] if len(slices) == 1 else stages[i].at[j]
                        add_into(g, got, self.at(k, *fixed))
                if i + 1 < len(axes):
                    nxt = axes[i + 1]
                    self.send(nxt, [2] if nxt == "y" else slices, fixed, stages[i + 1])
                    yield
            if "z" in axes:
                far = [((z // 2 + k) % (nz // 2)) for k in range(1, nz // 2)]
                parts = [(dev(c, y, b, f * 2 + z % 2), fixed + [f]) for f in far]
                own = fixed + [z // 2]
            else:
                far = [(z + k) % nz for k in range(1, nz)]
                parts = [(dev(c, y, b, f), fixed + [f % 2, f // 2]) for f in far]
                own = fixed + [z % 2, z // 2]
            for k, (to, at) in enumerate(parts):
                self.start(g.at[self.at(3, *at)], rz.at[m, h, k], to)
            yield
            self.wait()
            total = g[self.at(3, *own)].astype(F32)
            for k in range(len(parts)):
                total = total + rz[m, h, k].astype(F32)
            at = (slice(None), slice(h * lanes2, (h + 1) * lanes2))
            self.out[0][at] = total
            results.append(load(self.out[0].at[at], self.out[1].at[at]))

    class WholeSum(Sum):
        def __init__(self, key, grad, rcv, rcv1, rcvz, out, result):
            self.direct = key in DIRECT
            self.refs = (grad, rcv, rcv1, rcvz, out)
            self.result = result

        def steps(self):
            grad, rcv, rcv1, rcvz, out = self.refs
            self.cps = []
            if self.direct:
                for k, (py, pb) in enumerate([(y, b)] + xy_peers):
                    self.start(grad.at[co, py * 2 + pb], rcv.at[k], dev(co, py, pb))
            else:
                self.start(grad.at[co], rcv, core_dev)
                yield
                self.wait()
                for i in range(4):
                    add_into(grad, rcv.at[i], (c, i))
            for k, (py, pb) in enumerate(xy_peers):
                self.start(grad.at[c, py * 2 + pb], rcv1.at[k], dev(c, py, pb))
            yield
            self.wait()
            total = grad[c, xy].astype(F32)
            for k in range(3):
                total = total + rcv1[k].astype(F32)
            if self.direct:
                for k in range(4):
                    total = total + rcv[k].astype(F32)
            rcvz[z] = total.astype(grad.dtype)
            for k in range(1, nz):
                self.start(rcvz.at[z], rcvz.at[z], dev(c, y, b, (z + k) % nz))
            yield
            self.wait()
            total = rcvz[0].astype(F32)
            for k in range(1, nz):
                total = total + rcvz[k].astype(F32)
            out[c, xy] = total.astype(grad.dtype)
            for py, pb in xy_peers:
                self.start(out.at[c, xy], out.at[c, xy], dev(c, py, pb))
            if self.direct:
                for py, pb in [(y, b)] + xy_peers:
                    self.start(out.at[c, xy], out.at[c, xy], dev(co, py, pb))
            else:
                yield
                self.wait()
                self.start(out.at[c], out.at[c], core_dev)
            yield
            self.wait()
            results.append(load(out, self.result))

    chains = {}
    feeds = {}
    for m, (name, out) in enumerate((("d", (o_down, h_down)), ("u", (o_up, h_up)))):
        for h in range(2):
            key = name + str(h)
            feeds[key] = FeedSum(m, h, AXES[key], out)

    def point(name):
        for key in SCHEDULE.get(name, ()):
            if key == "m":
                send_mixed_y.pop(0).start()
            else:
                if key not in chains:
                    chains[key] = feeds[key].steps()
                next(chains[key], None)

    order = (t_d, t_c, t_y, t)

    def feed_grad(m, k, left, right):
        out = mm(left, right, 0, 0).astype(BF16)
        for h in range(2):
            for zz in range(nz):
                for bb in range(2):
                    i = (zz * 2 + bb) * fr
                    at = {"x": bb, "z": zz % 2}
                    at = tuple(at[a] for a in feeds["du"[m] + str(h)].free)
                    g[(m, h, k) + at + (zz // 2,)] = out[i:i + fr, h * lanes2:(h + 1) * lanes2]

    point("n2")

    for k, j in enumerate(order):
        feed_grad(0, k, gb[...], hid[j])
        if k < 2:
            feeds["d0"].send_core(k)
            feeds["d1"].send_core(k)
        point("dk" + str(k))

    def feed_back(k, j):
        for i in range(n // tile_h):
            at = slice(i * tile_h, (i + 1) * tile_h)
            gp = (slope[j, at, :].astype(F32) * mm(gb[at, :], wb[1, j], 1, 1)).astype(BF16)
            slope[j, at, :] = gp
            g2[at, :] += mm(gp, wb[0, j])
        up_rows[k] = col_sum(slope[j].astype(F32))
        feed_grad(1, k, flow[...], slope[j])

    up_rows = [None] * blocks
    for k, j in enumerate(order):
        feed_back(k, j)
        if k < 2:
            feeds["u0"].send_core(k)
            feeds["u1"].send_core(k)
        point("uk" + str(k))
    for k, j in enumerate(order):
        i = look + S_UP + j
        gs[i // 64, (i // 16) % 4, pl.ds(i % 16, 1), :] = up_rows[k]

    def first_back(i, carry):
        at = pl.ds(pl.multiple_of(i * padded, padded), padded)
        acc = g2[at, :]
        nn = en[at, :]
        add_row(S_GAIN1, col_sum(acc * nn))
        add_row(S_SHIFT1, col_sum(acc))
        gg = acc * vec[GAIN1]
        inv = inv1[at, 0:1]
        back = inv * (gg - row_mean(gg) - nn * row_mean(gg * nn))
        ga = back.astype(BF16)
        hid[0, at, :] = ga
        gm = mm(ga, wo[...], 1, 1)
        gb[at, :] = (gm * rinv[at, :].astype(F32)).astype(BF16)
        return carry

    lax.fori_loop(0, blocks, first_back, 0, unroll=True)
    point("n1")

    ga = hid.at[0]
    out_grad = mm(mx[...], ga[...], 0, 0).astype(BF16)
    for i in range(8):
        r = width // 8
        go[i // 4, i % 4] = out_grad[i * r:(i + 1) * r]
    chains["O"] = WholeSum("O", go, gorc, gor1, gorz, o_out, h_out).steps()
    next(chains["O"])
    small = mm(xa[:, 0:128], ga[...], 0, 0)
    for i in range(8):
        gs[i // 4, i % 4] += small[16 * i:16 * i + 16]
    chains["S"] = WholeSum("S", gs, gsrc, gsr1, gsrz, o_small, h_small).steps()
    next(chains["S"])
    point("og")

    tile_b = n // 2

    def attend_back(p):
        lanes = pl.ds(p * 128, 128)
        qt[...] = qkv[p, :, 0:128].T
        dt[...] = gb[:, lanes].T
        for h in range(2):
            def tile(i, carry):
                at = pl.ds(pl.multiple_of(i * tile_b, tile_b), tile_b)
                d = gb[at, lanes]
                own = (lane // 64) == h
                dm = jnp.where(own, d, jnp.zeros_like(d))
                centre = jnp.sum(
                    jnp.where(own, d.astype(F32) * mxf[at, lanes], 0.0), axis=1, keepdims=True
                )
                s = (mm(dm, qkv[p, :, 256:384], 1, 1) - centre).astype(BF16)
                s = s * prob[2 * p + h, at, :]
                ds[at, :] = s
                dq = mm(s, qkv[p, :, 128:256])
                if h == 0:
                    mxf[at, lanes] = jnp.where(lane < 64, dq, mxf[at, lanes])
                else:
                    rinv[at, lanes] = jnp.where(lane < 64, mxf[at, lanes], dq).astype(BF16)
                return carry

            lax.fori_loop(0, n // tile_b, tile, 0, unroll=True)
            half = slice(64 * h, 64 * h + 64)
            dk = mm(qt[half, :], ds[...])
            dv = mm(dt[half, :], prob[2 * p + h])
            qt[half, :] = dk.astype(BF16)
            dt[half, :] = dv.astype(BF16)
            point("a" + str(p) + "ab"[h])
        qkv[p, :, 0:128] = rinv[:, lanes]
        qkv[p, :, 128:256] = qt[...].T
        qkv[p, :, 256:384] = dt[...].T
        grad = mm(xa[:, 0:128], qkv[p, :, 0:384], 0, 0).astype(BF16)
        for i in range(8):
            gp_[p, i // 4, i % 4] = grad[16 * i:16 * i + 16]
        key = "p" + str(p)
        chains[key] = WholeSum(
            key, gp_.at[p], gprc.at[p], gpr1.at[p], gprz.at[p], o_pairs.at[p], h_pairs.at[p]
        ).steps()
        next(chains[key])
        point("a" + str(p) + "w")

    attend_back(0)
    attend_back(1)
    attend_back(2)
    attend_back(3)

    out = mm(we[...], ga[...], 1, 1)
    for p in range(pairs):
        out = out + mm(w2[1 + p, 0:look, 0:384], qkv[p, :, 0:384], 1, 1)
    for i in range(blocks):
        xs[i, 0:look, :] = out[:, i * padded:i * padded + rows].astype(BF16)
    own_s = sems.local(xs.at[t, 0:look], o_series.at[t])
    own_s.start()
    send_s = []
    for k in range(1, blocks):
        other = (t + k) % blocks
        send_s.append(sems.copy(xs.at[other, 0:look], o_series.at[t], (dp, other)))
    for cp in send_s:
        cp.start()
    point("sb")
    point("end")
    while send_mixed_y:
        send_mixed_y.pop(0).start()
    for _ in range(6):
        for key in chains:
            next(chains[key], None)
    for cp in send_s + send_mixed:
        cp.wait()
    for cp in results + [own_s, own_mixed]:
        cp.wait()


def finish(cfg, *refs):
    pairs, n_in, n_out = cfg
    inputs, refs = refs[:n_in], refs[n_in:]
    results, refs = refs[:n_out], refs[n_out:]
    held, refs = refs[:n_in], refs[n_in:]
    made, (sem_in, sem_out) = refs[:-2], refs[-2:]
    mixed, sgrad, up, down, pair_sums, out, small, we, wq, wk, wv, be = held
    made = (mixed, sgrad, up, down) + tuple(made)
    loads = [
        pltpu.make_async_copy(src, dst, sem_in.at[i])
        for i, (src, dst) in enumerate(zip(inputs, held))
    ]
    stores = [
        pltpu.make_async_copy(src, dst, sem_out.at[i])
        for i, (src, dst) in enumerate(zip(made, results))
    ]
    o_q, o_k, o_v, o_o, o_we, o_be, o_bq, o_bv, o_bo, o_g1, o_s1, o_bu, o_bd, o_g2, o_s2 = made[4:]
    for i in (4, 7, 11, 8, 5, 0, 1, 2, 3, 9, 10, 6):
        loads[i].start()
    look, width = we.shape
    r = width // 8
    for i in (4, 7, 11):
        loads[i].wait()
    row = lax.broadcasted_iota(jnp.int32, (128, 1), 0)
    b_high = be[...].astype(BF16).astype(F32)
    left = pad_rows(we[...].astype(F32), 128)
    left = left + jnp.where(row == look, b_high, 0.0)
    left = (left + jnp.where(row == look + 1, be[...] - b_high, 0.0)).astype(BF16)
    total = jnp.zeros((128, width), F32)
    for j, (o, w) in enumerate(((o_q, wq), (o_k, wk), (o_v, wv))):
        sums = jnp.concatenate(
            [
                jnp.concatenate(
                    [pair_sums[p, i // 4, i % 4, :, 128 * j:128 * j + 128] for i in range(8)],
                    axis=0,
                ).astype(F32)
                for p in range(pairs)
            ],
            axis=1,
        )
        if j == 0:
            sums = sums * 0.125
        last = sums[look:look + 1]
        o[...] = mm(left, (sums + jnp.where(row == look + 1, last, 0.0)).astype(BF16), 0, 0)
        stores[4 + j].start()
        if j == 0:
            o_bq[...] = last
        if j == 2:
            o_bv[...] = last
        loads[8 + j].wait()
        total = total + mm(sums.astype(BF16), w[...], 1, 1)
        if j == 0:
            loads[5].wait()
            for i in range(8):
                o_o[i * r:(i + 1) * r, :] = out[i // 4, i % 4].astype(F32)
            stores[7].start()
            for i in range(4):
                loads[i].wait()
                stores[i].start()
    loads[6].wait()
    total = total + jnp.concatenate([small[i // 4, i % 4] for i in range(8)], axis=0)
    o_we[...] = total[:look]
    o_be[...] = total[look:look + 1]

    def vector(i):
        i = look + i
        return small[i // 64, (i // 16) % 4, i % 16:i % 16 + 1, :]

    o_bo[...] = vector(0)
    for o, i in (
        (o_g1, S_GAIN1), (o_s1, S_SHIFT1), (o_bd, S_DOWN), (o_g2, S_GAIN2), (o_s2, S_SHIFT2)
    ):
        o[...] = vector(i)
    for i in range(4):
        o_bu[:, i * width:(i + 1) * width] = vector(S_UP + i)
    for cp in stores[8:]:
        cp.start()
    for cp in stores:
        cp.wait()


def body(
    series, embed_weight, embed_bias, query_weight, query_bias, key_weight, value_weight,
    value_bias, out_weight, out_bias, first_gain, first_shift, up_weight, up_bias,
    down_weight, down_bias, second_gain, second_shift, cotangent,
    *, dp_size, tensor_size,
):
    windows, rows, look = series.shape
    width = embed_weight.shape[1]
    hidden = up_weight.shape[0]
    pairs = HEADS // 2
    assert windows == tensor_size == 4 and width == hidden == HEADS * 64
    assert dp_size % 4 == 0 and look % 16 == 0 and look + S_UP + 4 <= 128
    padded = -(-rows // 32) * 32
    n = tensor_size * padded
    nz = dp_size // 2
    fr = width // dp_size
    r = width // 8
    half = hidden // 2

    def scr(*shape, dtype=BF16):
        return pltpu.VMEM(shape, dtype)

    scratch = [
        scr(4, 128, rows),
        scr(n, 256),
        scr(n, width, dtype=F32),
        scr(pairs, n, 512),
        scr(HEADS, n, n),
        scr(n, n),
        scr(n, width, dtype=F32),
        scr(n, width),
        scr(n, width),
        scr(n, 128, dtype=F32),
        scr(n, width),
        scr(4, n, hidden),
        scr(4, n, hidden),
        scr(4, rows, width),
        scr(n, width, dtype=F32),
        scr(n, width),
        scr(128, n),
        scr(128, n),
        scr(2, 4, hidden, width),
        scr(pairs, width, 384),
        scr(width, width),
        scr(look, width),
        scr(1 + pairs, 256, width),
        scr(4, 8, hidden, dtype=F32),
        scr(2, 2, 4, 2, 2, nz // 2, fr, half),
        scr(2, 2, 2, 2, 2, nz // 2, fr, half),
        scr(2, 2, 2, 2, nz // 2, fr, half),
        scr(2, 2, 2, nz // 2, fr, half),
        scr(2, 2, nz // 2, fr, half),
        scr(2, 2, nz - 1, fr, half),
        scr(pairs, 2, 4, 16, 384),
        scr(pairs, 4, 16, 384),
        scr(pairs, 3, 16, 384),
        scr(pairs, nz, 16, 384),
        scr(2, 4, r, width),
        scr(4, r, width),
        scr(3, r, width),
        scr(nz, r, width),
        scr(2, 4, 16, width, dtype=F32),
        scr(4, 16, width, dtype=F32),
        scr(3, 16, width, dtype=F32),
        scr(nz, 16, width, dtype=F32),
        scr(pairs, 2, 4, 16, 384),
        scr(2, 4, r, width),
        scr(2, 4, 16, width, dtype=F32),
        scr(fr, hidden, dtype=F32),
        scr(fr, hidden, dtype=F32),
        scr(9, 1, width, dtype=F32),
        scr(1, hidden),
        scr(8, hidden, dtype=F32),
        pltpu.SemaphoreType.DMA((N_SEND + N_SEND_Z * nz,)),
        pltpu.SemaphoreType.DMA((N_RECV + N_RECV_Z * nz,)),
    ]
    hbm = pl.BlockSpec(memory_space=pl.ANY)
    vmem = pl.BlockSpec(memory_space=pltpu.VMEM)
    sd = jax.ShapeDtypeStruct
    bias = embed_bias.reshape(1, -1)
    mixed, sgrad, g_pairs, g_out, g_small, g_up, g_down = pl.pallas_call(
        functools.partial(kernel, (4, rows, padded, nz, fr)),
        out_shape=[
            sd((4, rows, width), BF16),
            sd((4, look, rows), BF16),
            sd((pairs, 2, 4, 16, 384), BF16),
            sd((2, 4, r, width), BF16),
            sd((2, 4, 16, width), F32),
            sd((fr, hidden), F32),
            sd((fr, hidden), F32),
        ],
        in_specs=[hbm] * 19,
        out_specs=[hbm] * 7,
        scratch_shapes=scratch,
        compiler_params=pltpu.CompilerParams(
            collective_id=1, has_side_effects=True, vmem_limit_bytes=64 * 1024 * 1024
        ),
    )(
        jnp.swapaxes(series, 1, 2), cotangent, embed_weight, query_weight, key_weight,
        value_weight, out_weight, up_weight, down_weight, bias,
        *(v.reshape(1, -1) for v in (
            query_bias, value_bias, out_bias, first_gain, first_shift, down_bias,
            second_gain, second_shift, up_bias,
        )),
    )
    vector = sd((1, width), F32)
    operands = (
        mixed, sgrad, g_up, g_down, g_pairs, g_out, g_small, embed_weight, query_weight,
        key_weight, value_weight, bias,
    )
    made = [
        *[sd((width, width), F32)] * 4,
        sd((look, width), F32),
        *[vector] * 6,
        sd((1, 4 * hidden), F32),
        *[vector] * 3,
    ]
    out = pl.pallas_call(
        functools.partial(finish, (pairs, len(operands), 4 + len(made))),
        out_shape=[sd(a.shape, a.dtype) for a in operands[:4]] + made,
        in_specs=[hbm] * len(operands),
        out_specs=[hbm] * (4 + len(made)),
        scratch_shapes=[
            *[scr(*a.shape, dtype=a.dtype) for a in operands],
            *[scr(*a.shape, dtype=a.dtype) for a in made],
            pltpu.SemaphoreType.DMA((len(operands),)),
            pltpu.SemaphoreType.DMA((4 + len(made),)),
        ],
        compiler_params=pltpu.CompilerParams(vmem_limit_bytes=64 * 1024 * 1024),
    )(*operands)
    mixed, sgrad, g_up, g_down, g_q, g_k, g_v, g_o, g_e = out[:9]
    g_be, g_bq, g_bv, g_bo, g_g1, g_s1, g_bu, g_bd, g_g2, g_s2 = (
        v.reshape(-1) for v in out[9:]
    )
    return (
        mixed, jnp.swapaxes(sgrad, 1, 2), g_e, g_be, g_q, g_bq, g_k, g_v, g_bv, g_o, g_bo,
        g_g1, g_s1, g_up.T, g_bu, g_down.T, g_bd, g_g2, g_s2,
    )


def solution(mesh):
    token = P("dp", "tensor", None)
    return jax.shard_map(
        functools.partial(
            body, dp_size=mesh.shape["dp"], tensor_size=mesh.shape["tensor"]
        ),
        mesh=mesh,
        in_specs=(
            token, P(), P(), P(), P(), P(), P(), P(), P(), P(), P(), P(),
            P("tensor", None), P("tensor"), P("tensor", None), P(), P(), P(), token,
        ),
        out_specs=(
            token, token, P(), P(), P(), P(), P(), P(), P(), P(), P(), P(), P(),
            P("tensor", "dp"), P(), P("tensor", "dp"), P(), P(), P(),
        ),
        check_vma=False,
    )
```
